512 devices in a mesh: section: 2 (over core), seq: 64 (over z, y), mp: 4 (over x).
Axes of the slice: x: 4, y: 4, z: 16, core: 2. Of those that a mesh axis runs over, the one named last changes fastest.
Arguments:
- span_states: bfloat16 [8192, 4096], P('seq', ('section', 'mp')), may hold values from -6 to 6
- queries: bfloat16 [8192, 4096], P('seq', ('section', 'mp')), may hold values from -6 to 6
- slot_span: int32 [128], P('seq'), may hold values from 0 to 127, as said below
- neighbour_ids: int32 [128, 256], P('seq'), may hold values from 0 to 63999, as said below
- neighbour_count: int32 [128], P('seq'), may hold values from 1 to 2
- table: bfloat16 [64000, 896], P('seq'), may hold values from -6 to 6
- cond_weight: bfloat16 [4096, 896], P(('section', 'mp')), may hold values from -0.09375 to 0.09375
- kv_weight: bfloat16 [896, 2, 4096], P(None, None, ('section', 'mp')), may hold values from -0.1875 to 0.1875
Outputs:
- attended: bfloat16 [8192, 4096], P('seq', ('section', 'mp'))
The draws below stay inside these ranges and needn't reach their ends.
Inputs may be any that keep to these rules, and one draw needn't show every extreme that they name: `slot_span`: A permutation of the 128 spans. The 2 slots of seq index i hold spans c with c // 2 equal to i - 1, i or i + 1 (cyclically over the seq indices), at most 1 from each side. `neighbour_ids`: over the spans of one seq index (c // 2 fixed), the ids at the 32 positions of one index g of section and mp (positions g * 32 to g * 32 + 31) fall at most 2 times into one block of 1000 consecutive ids, a bound that is reached; within one span at most once.
All inputs are finite; a program needn't handle non-finite values.
Results may differ from the reference program's by a relative error of at most 0.013.
Values may be sent and summed in bfloat16 or wider, within the bound.
A program may use at most 64 MiB of HBM per device.

```python
import math
import jax
import jax.numpy as jnp
from jax import lax

D = 4096
HD = 128
HEADS = 32
E = 896
EHD = 128
SPAN = 64
NEIGH = 2
NLEN = 128
ROWS = 256
CH_DEV = 2
VOCAB_DEV = 1000
TOKENS = 8192
SPANS = 128
VOCAB = 64000
PART = 32


def draw_slot_span(key, part):
    key = jax.random.fold_in(key, 11)
    shards = SPANS // CH_DEV
    half_count = CH_DEV // 2
    pair_key, order_key = jax.random.split(key)
    crossing = jax.random.randint(pair_key, (shards,), 0, half_count + 1)
    crossing = crossing.at[0].set(half_count)
    incoming = jnp.roll(crossing, 1)
    position = jnp.arange(CH_DEV)[None, :]
    moves = jnp.where(position < incoming[:, None], -1, jnp.where(position >= CH_DEV - crossing[:, None], 1, 0))
    owners = jnp.mod(jnp.arange(shards)[:, None] + moves, shards).reshape(-1)
    shuffle = jax.random.permutation(order_key, SPANS)
    order = jnp.argsort(owners * SPANS + shuffle, stable=True)
    return order.astype(jnp.int32)


def draw_neighbour_ids(key, part):
    key = jax.random.fold_in(key, 12)
    shards = SPANS // CH_DEV
    groups = ROWS // PART
    rot_key, mix_key, row_key = jax.random.split(key, 3)
    rotation = jax.random.randint(rot_key, (shards, 1, groups, 1), 0, shards)
    owners = jnp.mod(jnp.arange(PART)[None, None, None, :] + rotation, shards)
    owners = jnp.broadcast_to(owners, (shards, CH_DEV, groups, PART))
    mixing = jax.random.randint(mix_key, (shards, CH_DEV, groups, PART), 0, PART) * PART + jnp.arange(PART)
    order = jnp.argsort(mixing, axis=-1, stable=True)
    owners = jnp.take_along_axis(owners, order, axis=-1)
    rows_in = jax.random.randint(row_key, (shards, CH_DEV, groups, PART), 0, VOCAB_DEV)
    return (owners * VOCAB_DEV + rows_in).reshape(SPANS, ROWS).astype(jnp.int32)


def place_ends(entries, stream_key, smallest, largest):
    dims = entries.shape
    index_at = [jax.random.randint(jax.random.fold_in(stream_key, axis), (), 0, dims[axis]) for axis in range(len(dims))]
    entries = entries.at[tuple(index_at)].set(smallest)
    longest = dims.index(max(dims))
    index_at[longest] = (index_at[longest] + 1) % dims[longest]
    return entries.at[tuple(index_at)].set(largest)


def shard_levels(rng, shape, cuts, low, high):
    def one(dim, parts):
        draws = jax.random.uniform(jax.random.fold_in(jax.random.fold_in(rng, 6), dim), (parts,), jnp.float32, low / len(cuts), high / len(cuts))
        return jnp.repeat(jnp.exp(draws), shape[dim] // parts).reshape((-1,) + (1,) * (len(shape) - dim - 1))

    loudness = one(*cuts[0])
    for cut in cuts[1:]:
        loudness = loudness * one(*cut)
    return loudness


def centred(rng, shape, scale, most, pieces=(), kind=jnp.bfloat16):
    factor_of = shard_levels(rng, shape, pieces, -0.22, 0.18) if pieces else 1.0
    array = jax.random.normal(rng, shape, jnp.float32) * scale * factor_of
    return jnp.minimum(jnp.maximum(array, -most), most).astype(kind)


def setup_inputs(seed: int = 0) -> dict:
    streams_of = jax.random.split(jax.random.key(seed), 9)
    return {
        "span_states": centred(streams_of[0], (TOKENS, D), 1.0, 6.0, ((0, 64), (1, 8))),
        "queries": centred(streams_of[1], (TOKENS, D), 1.0, 6.0, ((0, 64), (1, 8))),
        "slot_span": draw_slot_span(jax.random.fold_in(streams_of[8], 71), 0),
        "neighbour_ids": draw_neighbour_ids(jax.random.fold_in(streams_of[8], 71), 0),
        "neighbour_count": place_ends(jax.random.randint(streams_of[4], (SPANS,), 1, NEIGH + 1), jax.random.fold_in(streams_of[4], 1), 1, NEIGH).astype(jnp.int32),
        "table": centred(streams_of[5], (VOCAB, E), 1.0, 6.0, ((0, 64),)),
        "cond_weight": centred(streams_of[6], (D, E), D ** -0.5, 0.09375, ((0, 8),)),
        "kv_weight": centred(streams_of[7], (E, 2, D), E ** -0.5, 0.1875, ((2, 8),)),
    }


def encode(embedded, condition):
    head_count = embedded.shape[-1] // EHD
    query_h = embedded.astype(jnp.float32).reshape(-1, head_count, EHD)
    key_h = condition.astype(jnp.float32).reshape(-1, head_count, EHD)
    scores = jnp.einsum('phd,lhd->hpl', query_h, key_h) / math.sqrt(EHD)
    weights = jax.nn.softmax(scores, axis=-1).astype(jnp.bfloat16)
    attended_rows = jnp.einsum('hpl,lhd->phd', weights.astype(jnp.float32), key_h)
    return (embedded.astype(jnp.float32) + attended_rows.reshape(embedded.shape)).astype(jnp.bfloat16)

def reference(span_states, queries, slot_span, neighbour_ids, neighbour_count, table, cond_weight, kv_weight):
    states = span_states.reshape(SPANS, SPAN, D)
    query_rows = queries.reshape(SPANS, SPAN, D)
    slot_ids = jnp.take(neighbour_ids, slot_span, axis=0)
    slot_counts = jnp.take(neighbour_count, slot_span, axis=0)
    kv_full = kv_weight.astype(jnp.float32)
    row_groups = jnp.arange(ROWS, dtype=jnp.int32) // NLEN

    def one_span(items):
        state, query, ids, count = items
        condition = jnp.dot(state, cond_weight, preferred_element_type=jnp.float32).astype(jnp.bfloat16)
        embedded = jnp.take(table, ids, axis=0)
        encoded = encode(embedded, condition)
        key_value = jnp.einsum('re,ekf->rkf', encoded.astype(jnp.float32), kv_full).astype(jnp.bfloat16)
        query_h = query.astype(jnp.float32).reshape(SPAN, HEADS, HD)
        key_h = key_value[:, 0].astype(jnp.float32).reshape(ROWS, HEADS, HD)
        value_h = key_value[:, 1].astype(jnp.float32).reshape(ROWS, HEADS, HD)
        scores = jnp.einsum('lhd,rhd->hlr', query_h, key_h) / math.sqrt(HD)
        valid = row_groups < count
        scores = jnp.where(valid[None, None, :], scores, -jnp.inf)
        weights = jax.nn.softmax(scores, axis=-1).astype(jnp.bfloat16)
        output = jnp.einsum('hlr,rhd->lhd', weights.astype(jnp.float32), value_h)
        return output.reshape(SPAN, D).astype(jnp.bfloat16)
    result = lax.map(one_span, (states, query_rows, slot_ids, slot_counts))
    return result.reshape(TOKENS, D)
```

```python
import functools
import math

import jax
import jax.numpy as jnp
from jax import lax
from jax.experimental import pallas as pl
from jax.experimental.pallas import tpu as pltpu
from jax.sharding import PartitionSpec as P

HD = 128
LANES = 128
TILE = 16
BF16 = jnp.bfloat16
F32 = jnp.float32
MESH = pl.DeviceIdType.MESH


def to_column(row, rows):
    shape = (rows, row.shape[1])
    here = lax.broadcasted_iota(jnp.int32, shape, 0) == lax.broadcasted_iota(jnp.int32, shape, 1)
    return jnp.sum(jnp.where(here, row, 0.0), axis=1, keepdims=True)


def lane_sum(mask, values):
    return jnp.sum(jnp.where(mask, values, 0.0), axis=1, keepdims=True)


def kernel(
    sizes,
    slot_span,
    counts,
    ids,
    states_hbm,
    queries_hbm,
    table_hbm,
    cond_weight_hbm,
    kv_hbm,
    out,
    states,
    queries,
    table,
    cond_weight,
    kv_raw,
    kv_weight,
    kv_f32,
    facts,
    asked_f32,
    answers,
    arrived,
    picks,
    partial,
    partial_out,
    partial_in,
    condition,
    encoded,
    local_sems,
    facts_sems,
    row_sems,
    part_sems,
    cond_sems,
    enc_send,
    enc_recv,
):
    shards, sections, mps, spans, part, span_len = sizes
    groups = sections * mps
    enc_width = table.shape[1]
    heads = enc_width // LANES
    vocab = table.shape[0]
    me = lax.axis_index("seq")
    section = lax.axis_index("section")
    mp = lax.axis_index("mp")
    group = section * mps + mp

    loads = [
        pltpu.make_async_copy(src, dst, local_sems.at[n])
        for n, (src, dst) in enumerate(
            (
                (states_hbm, states),
                (cond_weight_hbm, cond_weight),
                (table_hbm, table),
                (kv_hbm, kv_raw),
                (queries_hbm, queries),
            )
        )
    ]
    for load in loads:
        load.start()

    def seq_peer(d):
        return {"seq": lax.rem(me + d, shards)}

    def group_peer(ds, dx):
        return {"section": lax.rem(section + ds, sections), "mp": lax.rem(mp + dx, mps)}

    group_steps = [(ds, dx) for ds in range(sections) for dx in range(mps)][1:]

    barrier = pltpu.get_barrier_semaphore()

    def greet(d, carry):
        pl.semaphore_signal(barrier, inc=1, device_id=seq_peer(d), device_id_type=MESH)
        return carry

    lax.fori_loop(1, shards, greet, 0)
    for ds, dx in group_steps:
        pl.semaphore_signal(barrier, inc=1, device_id=group_peer(ds, dx), device_id_type=MESH)

    lane = lax.broadcasted_iota(jnp.int32, (1, LANES), 1)
    chunks = ids.shape[1] // LANES
    per_chunk = LANES // part
    all_ids = ids[...]
    own_ids = all_ids[:, :LANES]
    for c in range(1, chunks):
        own_ids = jnp.where(group // per_chunk == c, all_ids[:, c * LANES : (c + 1) * LANES], own_ids)
    own_ids = pltpu.roll(own_ids, lax.rem(LANES - lax.rem(group, per_chunk) * part, LANES), 1)
    message = jnp.zeros((1, LANES), jnp.int32)
    for k in range(spans):
        line = own_ids[k : k + 1]
        if k:
            line = pltpu.roll(line, k * part, 1)
        message = jnp.where((lane >= k * part) & (lane < (k + 1) * part), line, message)
        message = jnp.where(lane == spans * part + k, slot_span[k], message)
        message = jnp.where(lane == spans * part + spans + k, counts[k], message)
    facts[0:1, :] = message

    pl.semaphore_wait(barrier, shards - 1 + len(group_steps))

    def tell(d, carry):
        pltpu.make_async_remote_copy(
            src_ref=facts.at[pl.ds(0, 1)],
            dst_ref=facts.at[pl.ds(shards - d, 1)],
            send_sem=facts_sems.at[0],
            recv_sem=facts_sems.at[1],
            device_id=seq_peer(d),
            device_id_type=MESH,
        ).start()
        return carry

    lax.fori_loop(1, shards, tell, 0)

    loads[0].wait()
    loads[1].wait()
    product = jnp.dot(states[...], cond_weight[...], preferred_element_type=F32)
    block_rows = product.shape[0] // groups
    partial[...] = product.reshape(groups, block_rows, enc_width)
    partial_out[...] = product.astype(BF16).reshape(groups, block_rows, enc_width)
    for n, (ds, dx) in enumerate(group_steps):
        to = lax.rem(section + ds, sections) * mps + lax.rem(mp + dx, mps)
        back = ((sections - ds) % sections) * mps + (mps - dx) % mps
        pltpu.make_async_remote_copy(
            src_ref=partial_out.at[to],
            dst_ref=partial_in.at[back],
            send_sem=part_sems.at[0],
            recv_sem=part_sems.at[1],
            device_id=group_peer(ds, dx),
            device_id_type=MESH,
        ).start()

    loads[3].wait()
    pairs = kv_weight.shape[1] // LANES
    step_rows = kv_f32.shape[0] // pairs

    def split_pairs(step, carry):
        rows = pl.ds(pl.multiple_of(step * step_rows * pairs, TILE), step_rows * pairs)
        kv_f32[...] = kv_raw[rows, :].astype(F32)
        for t in range(pairs // 2):
            for j in range(2):
                column = (j * (pairs // 2) + t) * LANES
                kv_weight[pl.ds(pl.multiple_of(step * step_rows, TILE), step_rows), column : column + LANES] = (
                    kv_f32[pl.ds(t * 2 + j, step_rows, stride=pairs), :].astype(BF16)
                )
        return carry

    asked_f32[...] = jnp.zeros_like(asked_f32)

    def await_bytes(ref, sems):
        pltpu.make_async_remote_copy(
            src_ref=ref, dst_ref=ref, send_sem=sems.at[0], recv_sem=sems.at[1], device_id=seq_peer(1), device_id_type=MESH
        ).wait()

    await_bytes(facts.at[pl.ds(1, shards - 1)], facts_sems)

    told = facts[...]
    told_f32 = told.astype(F32)
    wide = told.shape
    lanes = lax.broadcasted_iota(jnp.int32, wide, 1)
    rows_d = lax.broadcasted_iota(jnp.int32, wide, 0)
    local = told - me * vocab
    inside = (local >= 0) & (local < vocab)
    local_f32 = (local + 1).astype(F32)
    want_row = jnp.zeros((1, LANES), F32)
    for k in range(spans):
        want = lane_sum(inside & (lanes >= k * part) & (lanes < (k + 1) * part), local_f32)
        want_row += jnp.sum(jnp.where(lanes == rows_d + k * shards, want, 0.0), axis=0, keepdims=True)
    span_row = (lax.rem(me + lax.rem(lane, shards), shards) * spans + lane // shards).astype(F32)
    span_row = jnp.where(lane < spans * shards, span_row, -1.0)
    loads[2].wait()
    marks = []
    vocab_lane = lax.broadcasted_iota(jnp.int32, (shards, vocab), 1).astype(F32)
    for k in range(spans):
        slot_holds = lane_sum(lanes == spans * part + k, told_f32)
        request = lane_sum(span_row == slot_holds, want_row) - 1.0
        marks.append((vocab_lane == request).astype(F32).astype(BF16))
    rows_out = jnp.dot(jnp.concatenate(marks, axis=0), table[...], preferred_element_type=F32)
    for k in range(spans):
        for h in range(heads):
            asked_f32[pl.ds(k * heads + h, shards, stride=TILE), :] = rows_out[
                k * shards : (k + 1) * shards, h * LANES : (h + 1) * LANES
            ]
    answers[...] = asked_f32[...].astype(BF16).reshape(answers.shape)

    def answer(d, carry):
        pltpu.make_async_remote_copy(
            src_ref=answers.at[d],
            dst_ref=arrived.at[shards - d],
            send_sem=row_sems.at[0],
            recv_sem=row_sems.at[1],
            device_id=seq_peer(d),
            device_id_type=MESH,
        ).start()
        return carry

    lax.fori_loop(1, shards, answer, 0)
    arrived[0] = answers[0]

    await_bytes(partial_in.at[pl.ds(1, groups - 1)], part_sems)
    total = partial[group]
    for n in range(1, groups):
        total += partial_in[n].astype(F32)
    condition[group] = total.astype(BF16)
    for ds, dx in group_steps:
        pltpu.make_async_remote_copy(
            src_ref=condition.at[group],
            dst_ref=condition.at[group],
            send_sem=cond_sems.at[0],
            recv_sem=cond_sems.at[1],
            device_id=group_peer(ds, dx),
            device_id_type=MESH,
        ).start()

    lax.fori_loop(0, kv_weight.shape[0] // step_rows, split_pairs, 0)

    kept = []
    place_lane = lax.broadcasted_iota(jnp.int32, (part, shards * TILE), 1).astype(F32)
    row_span = lax.rem(me + rows_d[:, :1], shards) * spans
    for k in range(spans):
        held = slot_span[k]
        id_row = jnp.zeros((1, LANES), F32)
        count = jnp.zeros((1, 1), F32)
        for home in range(spans):
            chosen = jnp.sum(jnp.where(row_span + home == held, told_f32, 0.0), axis=0, keepdims=True)
            moved = pltpu.roll(chosen, (LANES - home * part) % LANES, 1) if home else chosen
            id_row += moved
            count += lane_sum(lane == spans * part + spans + home, chosen)
        kept.append(count)
        owner = jnp.floor((id_row + 0.5) * (1.0 / vocab))
        step = owner - me.astype(F32)
        step = jnp.where(step < 0, step + shards, step)
        column = to_column(step * TILE, part)
        for h in range(heads):
            r = k * heads + h
            picks[r * part : (r + 1) * part, :] = (place_lane == column + r).astype(F32).astype(BF16)

    await_bytes(condition.at[pl.ds(0, groups - 1)], cond_sems)
    await_bytes(arrived.at[pl.ds(1, shards - 1)], row_sems)

    embedded = jnp.dot(
        picks[...], arrived[...].reshape(shards * TILE, LANES), preferred_element_type=F32
    )
    embedded_bf16 = embedded.astype(BF16)
    cond = condition[...].reshape(spans, span_len, enc_width)
    scores = []
    for k in range(spans):
        for h in range(heads):
            r = k * heads + h
            scores.append(
                lax.dot_general(
                    embedded_bf16[r * part : (r + 1) * part],
                    cond[k, :, h * LANES : (h + 1) * LANES],
                    (((1,), (1,)), ((), ())),
                    preferred_element_type=F32,
                )
            )
    weights = softmax(jnp.concatenate(scores, axis=0) * (1.0 / math.sqrt(LANES)))
    for k in range(spans):
        for h in range(heads):
            r = k * heads + h
            added = jnp.dot(
                weights[r * part : (r + 1) * part],
                cond[k, :, h * LANES : (h + 1) * LANES],
                preferred_element_type=F32,
            )
            encoded[group, k * part : (k + 1) * part, h * LANES : (h + 1) * LANES] = (
                embedded[r * part : (r + 1) * part] + added
            ).astype(BF16)

    def pass_on(index, block, target):
        return pltpu.make_async_remote_copy(
            src_ref=encoded.at[block],
            dst_ref=encoded.at[block],
            send_sem=enc_send.at[index],
            recv_sem=enc_recv.at[index],
            device_id=target,
            device_id_type=MESH,
        )

    sent = []
    for dx in range(1, mps):
        sent.append(pass_on(dx, group, group_peer(0, dx)))
        sent[-1].start()
    sibling = [pass_on(mps, group, group_peer(1, 0))]
    sibling[0].start()
    for dx in range(1, mps):
        block = section * mps + lax.rem(mp + mps - dx, mps)
        sent[dx - 1].wait_recv()
        onward = pass_on(mps + dx, block, group_peer(1, 0))
        onward.start()
        sibling.append(onward)
    for copy in sibling:
        copy.wait_recv()
    for copy in sent + sibling:
        copy.wait_send()

    loads[4].wait()
    rows = encoded[...].reshape(groups * spans * part, enc_width)
    key_value = jnp.dot(rows, kv_weight[...], preferred_element_type=F32).astype(BF16)
    width = kv_weight.shape[1] // 2
    local_heads = width // HD
    key_value = key_value.reshape(groups, spans, part, 2 * width)
    scores = []
    for k in range(spans):
        keys = key_value[:, k].reshape(groups * part, 2 * width)
        for t in range(local_heads):
            scores.append(
                lax.dot_general(
                    queries[k * span_len : (k + 1) * span_len, t * HD : (t + 1) * HD],
                    keys[:, t * HD : (t + 1) * HD],
                    (((1,), (1,)), ((), ())),
                    preferred_element_type=F32,
                )
            )
    neighbour = lax.broadcasted_iota(jnp.int32, scores[0].shape, 1) // (groups * part // sections)
    scores = [
        jnp.where(neighbour.astype(F32) < kept[n // local_heads], s * (1.0 / math.sqrt(HD)), -jnp.inf)
        for n, s in enumerate(scores)
    ]
    weights = softmax(jnp.concatenate(scores, axis=0))
    for k in range(spans):
        values = key_value[:, k].reshape(groups * part, 2 * width)
        for t in range(local_heads):
            n = k * local_heads + t
            out[k * span_len : (k + 1) * span_len, t * HD : (t + 1) * HD] = jnp.dot(
                weights[n * span_len : (n + 1) * span_len],
                values[:, width + t * HD : width + (t + 1) * HD],
                preferred_element_type=F32,
            ).astype(BF16)


def softmax(scores):
    high = jnp.max(scores, axis=1, keepdims=True)
    raised = jnp.exp(scores - high)
    return (raised / jnp.sum(raised, axis=1, keepdims=True)).astype(BF16)


def per_device(
    mesh_shape, span_states, queries, slot_span, neighbour_ids, neighbour_count, table, cond_weight, kv_weight
):
    shards, sections, mps = mesh_shape["seq"], mesh_shape["section"], mesh_shape["mp"]
    groups = sections * mps
    spans = slot_span.shape[0]
    part = neighbour_ids.shape[1] // groups
    tokens, width = queries.shape
    vocab, enc_width = table.shape
    pairs = 2 * width // LANES
    kv_rows = (
        kv_weight.reshape(enc_width, 2, width // LANES, LANES)
        .transpose(0, 2, 1, 3)
        .reshape(enc_width * pairs, LANES)
    )
    vmem = pl.BlockSpec(memory_space=pltpu.VMEM)
    smem = pl.BlockSpec(memory_space=pltpu.SMEM)
    hbm = pl.BlockSpec(memory_space=pl.ANY)
    rows_14 = spans * (enc_width // LANES)
    block_rows = tokens // groups
    dma = pltpu.SemaphoreType.DMA
    return pl.pallas_call(
        functools.partial(kernel, (shards, sections, mps, spans, part, tokens // spans)),
        out_shape=jax.ShapeDtypeStruct(queries.shape, queries.dtype),
        in_specs=[smem, smem, vmem, hbm, hbm, hbm, hbm, hbm],
        out_specs=vmem,
        scratch_shapes=[
            pltpu.VMEM(span_states.shape, BF16),
            pltpu.VMEM(queries.shape, BF16),
            pltpu.VMEM(table.shape, BF16),
            pltpu.VMEM(cond_weight.shape, BF16),
            pltpu.VMEM(kv_rows.shape, BF16),
            pltpu.VMEM((enc_width, 2 * width), BF16),
            pltpu.VMEM((enc_width // 8 * pairs, LANES), F32),
            pltpu.VMEM((shards, LANES), jnp.int32),
            pltpu.VMEM((shards * TILE, LANES), F32),
            pltpu.VMEM((shards, TILE, LANES), BF16),
            pltpu.VMEM((shards, TILE, LANES), BF16),
            pltpu.VMEM((rows_14 * part, shards * TILE), BF16),
            pltpu.VMEM((groups, block_rows, enc_width), F32),
            pltpu.VMEM((groups, block_rows, enc_width), BF16),
            pltpu.VMEM((groups, block_rows, enc_width), BF16),
            pltpu.VMEM((groups, block_rows, enc_width), BF16),
            pltpu.VMEM((groups, spans * part, enc_width), BF16),
            dma((5,)),
            dma((2,)),
            dma((2,)),
            dma((2,)),
            dma((2,)),
            dma((2 * mps,)),
            dma((2 * mps,)),
        ],
        compiler_params=pltpu.CompilerParams(
            collective_id=0, has_side_effects=True, vmem_limit_bytes=50 * 1024 * 1024
        ),
    )(slot_span, neighbour_count, neighbour_ids, span_states, queries, table, cond_weight, kv_rows)


def solution(mesh):
    placed = (
        P("seq", ("section", "mp")),
        P("seq", ("section", "mp")),
        P("seq"),
        P("seq", None),
        P("seq"),
        P("seq", None),
        P(("section", "mp"), None),
        P(None, None, ("section", "mp")),
    )
    return jax.shard_map(
        functools.partial(per_device, dict(mesh.shape)),
        mesh=mesh,
        in_specs=placed,
        out_specs=P("seq", ("section", "mp")),
        check_vma=False,
    )
```

```python
import functools
import math

import jax
import jax.numpy as jnp
from jax import lax
from jax.experimental import pallas as pl
from jax.experimental.pallas import tpu as pltpu
from jax.sharding import PartitionSpec as P

HD = 128
LANES = 128
TILE = 16
BF16 = jnp.bfloat16
F32 = jnp.float32
MESH = pl.DeviceIdType.MESH


def to_column(row, rows):
    shape = (rows, row.shape[1])
    here = lax.broadcasted_iota(jnp.int32, shape, 0) == lax.broadcasted_iota(jnp.int32, shape, 1)
    return jnp.sum(jnp.where(here, row, 0.0), axis=1, keepdims=True)


def lane_sum(mask, values):
    return jnp.sum(jnp.where(mask, values, 0.0), axis=1, keepdims=True)


def kernel(
    sizes,
    slot_span_hbm,
    counts_hbm,
    ids_hbm,
    states_hbm,
    queries_hbm,
    table_hbm,
    cond_weight_hbm,
    kv_hbm,
    out,
    slot_span,
    counts,
    ids,
    states,
    queries,
    table,
    cond_weight,
    kv_raw,
    kv_weight,
    kv_f32,
    facts_near,
    facts_far,
    asked_f32,
    answers_near,
    answers_far,
    arrived,
    picks,
    partial,
    partial_out,
    partial_in,
    condition,
    encoded,
    local_sems,
    facts_sems,
    row_sems,
    part_sems,
    cond_sems,
    enc_send,
    enc_recv,
):
    shards, sections, mps, spans, part, span_len = sizes
    groups = sections * mps
    enc_width = table.shape[1]
    heads = enc_width // LANES
    vocab = table.shape[0]
    me = lax.axis_index("seq")
    section = lax.axis_index("section")
    mp = lax.axis_index("mp")
    group = section * mps + mp

    loads = [
        pltpu.make_async_copy(src, dst, local_sems.at[n])
        for n, (src, dst) in enumerate(
            (
                (states_hbm, states),
                (cond_weight_hbm, cond_weight),
                (table_hbm, table),
                (kv_hbm, kv_raw),
                (queries_hbm, queries),
                (ids_hbm, ids),
                (slot_span_hbm, slot_span),
                (counts_hbm, counts),
            )
        )
    ]
    for load in loads[5:] + loads[:5]:
        load.start()

    half, margin = shards // 2, shards // 4

    def seq_peer(d):
        return {"seq": lax.rem(me + d, shards)}

    def over_peers(low, high, act):
        def body(i, carry):
            act(half + (i + 1) // 2 * (1 - 2 * lax.rem(i, 2)))
            return carry

        lax.fori_loop(low, high, body, 0)

    def wait_in(ref, sem):
        pltpu.make_async_remote_copy(
            src_ref=ref, dst_ref=ref, send_sem=sem, recv_sem=sem, device_id=seq_peer(1), device_id_type=MESH
        ).wait_recv()

    def wait_out(ref, sem):
        pltpu.make_async_remote_copy(
            src_ref=ref, dst_ref=ref, send_sem=sem, recv_sem=sem, device_id=seq_peer(1), device_id_type=MESH
        ).wait_send()

    def group_peer(ds, dx):
        return {"section": lax.rem(section + ds, sections), "mp": lax.rem(mp + dx, mps)}

    group_steps = [(ds, dx) for ds in range(sections) for dx in range(mps)][1:]

    barrier = pltpu.get_barrier_semaphore()

    facts_near[...] = jnp.full(facts_near.shape, -1, jnp.int32)
    facts_far[...] = jnp.full(facts_far.shape, -1, jnp.int32)
    over_peers(
        0, shards - 1, lambda d: pl.semaphore_signal(barrier, inc=1, device_id=seq_peer(d), device_id_type=MESH)
    )
    for ds, dx in group_steps:
        pl.semaphore_signal(barrier, inc=1, device_id=group_peer(ds, dx), device_id_type=MESH)

    lane = lax.broadcasted_iota(jnp.int32, (1, LANES), 1)
    chunks = ids.shape[1] // LANES
    per_chunk = LANES // part
    for load in loads[5:]:
        load.wait()
    all_ids = ids[...]
    own_ids = all_ids[:, :LANES]
    for c in range(1, chunks):
        own_ids = jnp.where(group // per_chunk == c, all_ids[:, c * LANES : (c + 1) * LANES], own_ids)
    own_ids = pltpu.roll(own_ids, lax.rem(LANES - lax.rem(group, per_chunk) * part, LANES), 1)
    message = jnp.zeros((1, LANES), jnp.int32)
    for k in range(spans):
        line = own_ids[k : k + 1]
        if k:
            line = pltpu.roll(line, k * part, 1)
        message = jnp.where((lane >= k * part) & (lane < (k + 1) * part), line, message)
        message = jnp.where(lane == spans * part + k, slot_span[k], message)
        message = jnp.where(lane == spans * part + spans + k, counts[k], message)
    facts_near[0:1, :] = message

    pl.semaphore_wait(barrier, shards - 1 + len(group_steps))

    def tell(into, sem):
        def act(d):
            pltpu.make_async_remote_copy(
                src_ref=facts_near.at[pl.ds(0, 1)],
                dst_ref=into.at[pl.ds(shards - d, 1)],
                send_sem=facts_sems.at[0],
                recv_sem=sem,
                device_id=seq_peer(d),
                device_id_type=MESH,
            ).start()

        return act

    far_facts, far_rows = 2 * margin - 1, 2 * margin + 1
    over_peers(0, far_facts, tell(facts_far, facts_sems.at[1]))
    over_peers(far_facts, shards - 1, tell(facts_near, facts_sems.at[2]))

    loads[0].wait()
    loads[1].wait()
    product = jnp.dot(states[...], cond_weight[...], preferred_element_type=F32)
    block_rows = product.shape[0] // groups
    partial[...] = product.reshape(groups, block_rows, enc_width)
    partial_out[...] = product.astype(BF16).reshape(groups, block_rows, enc_width)
    for n, (ds, dx) in enumerate(group_steps):
        to = lax.rem(section + ds, sections) * mps + lax.rem(mp + dx, mps)
        back = ((sections - ds) % sections) * mps + (mps - dx) % mps
        pltpu.make_async_remote_copy(
            src_ref=partial_out.at[to],
            dst_ref=partial_in.at[back],
            send_sem=part_sems.at[0],
            recv_sem=part_sems.at[1],
            device_id=group_peer(ds, dx),
            device_id_type=MESH,
        ).start()

    loads[3].wait()
    pairs = kv_weight.shape[1] // LANES
    step_rows = kv_f32.shape[0] // pairs

    def split_pairs(step, carry):
        rows = pl.ds(pl.multiple_of(step * step_rows * pairs, TILE), step_rows * pairs)
        kv_f32[...] = kv_raw[rows, :].astype(F32)
        for t in range(pairs // 2):
            for j in range(2):
                column = (j * (pairs // 2) + t) * LANES
                kv_weight[pl.ds(pl.multiple_of(step * step_rows, TILE), step_rows), column : column + LANES] = (
                    kv_f32[pl.ds(t * 2 + j, step_rows, stride=pairs), :].astype(BF16)
                )
        return carry

    asked_f32[...] = jnp.zeros_like(asked_f32)

    wide = facts_near.shape
    lanes = lax.broadcasted_iota(jnp.int32, wide, 1)
    rows_d = lax.broadcasted_iota(jnp.int32, wide, 0)
    span_row = (lax.rem(me + lax.rem(lane, shards), shards) * spans + lane // shards).astype(F32)
    span_row = jnp.where(lane < spans * shards, span_row, -2.0)
    vocab_lane = lax.broadcasted_iota(jnp.int32, (shards, vocab), 1).astype(F32)

    def look_up(told, answers):
        told_f32 = told.astype(F32)
        local = told - me * vocab
        inside = (local >= 0) & (local < vocab)
        local_f32 = (local + 1).astype(F32)
        want_row = jnp.zeros((1, LANES), F32)
        for k in range(spans):
            want = lane_sum(inside & (lanes >= k * part) & (lanes < (k + 1) * part), local_f32)
            want_row += jnp.sum(jnp.where(lanes == rows_d + k * shards, want, 0.0), axis=0, keepdims=True)
        marks = []
        for k in range(spans):
            slot_holds = lane_sum(lanes == spans * part + k, told_f32)
            request = lane_sum(span_row == slot_holds, want_row) - 1.0
            marks.append((vocab_lane == request).astype(F32).astype(BF16))
        rows_out = jnp.dot(jnp.concatenate(marks, axis=0), table[...], preferred_element_type=F32)
        for k in range(spans):
            for h in range(heads):
                asked_f32[pl.ds(k * heads + h, shards, stride=TILE), :] = rows_out[
                    k * shards : (k + 1) * shards, h * LANES : (h + 1) * LANES
                ]
        answers[...] = asked_f32[...].astype(BF16).reshape(answers.shape)

    def answer(answers):
        def act(d):
            pltpu.make_async_remote_copy(
                src_ref=answers.at[d],
                dst_ref=arrived.at[shards - d],
                send_sem=row_sems.at[0],
                recv_sem=row_sems.at[1],
                device_id=seq_peer(d),
                device_id_type=MESH,
            ).start()

        return act

    loads[2].wait()
    wait_in(facts_near.at[pl.ds(0, shards - 1 - far_facts)], facts_sems.at[2])
    near = facts_near[...]
    look_up(near, answers_near)
    over_peers(far_rows, shards - 1, answer(answers_near))
    arrived[0] = answers_near[0]
    wait_in(facts_far.at[pl.ds(0, far_facts)], facts_sems.at[1])
    look_up(jnp.where((rows_d > half - margin) & (rows_d < half + margin), facts_far[...], near), answers_far)
    over_peers(0, far_rows, answer(answers_far))
    told_f32 = near.astype(F32)

    wait_in(partial_in.at[pl.ds(1, groups - 1)], part_sems.at[1])
    total = partial[group]
    for n in range(1, groups):
        total += partial_in[n].astype(F32)
    condition[group] = total.astype(BF16)
    for ds, dx in group_steps:
        pltpu.make_async_remote_copy(
            src_ref=condition.at[group],
            dst_ref=condition.at[group],
            send_sem=cond_sems.at[0],
            recv_sem=cond_sems.at[1],
            device_id=group_peer(ds, dx),
            device_id_type=MESH,
        ).start()

    lax.fori_loop(0, kv_weight.shape[0] // step_rows, split_pairs, 0)

    kept = []
    place_lane = lax.broadcasted_iota(jnp.int32, (part, shards * TILE), 1).astype(F32)
    row_span = lax.rem(me + rows_d[:, :1], shards) * spans
    for k in range(spans):
        held = slot_span[k]
        id_row = jnp.zeros((1, LANES), F32)
        count = jnp.zeros((1, 1), F32)
        for home in range(spans):
            chosen = jnp.sum(jnp.where(row_span + home == held, told_f32, 0.0), axis=0, keepdims=True)
            moved = pltpu.roll(chosen, (LANES - home * part) % LANES, 1) if home else chosen
            id_row += moved
            count += lane_sum(lane == spans * part + spans + home, chosen)
        kept.append(count)
        owner = jnp.floor((id_row + 0.5) * (1.0 / vocab))
        step = owner - me.astype(F32)
        step = jnp.where(step < 0, step + shards, step)
        column = to_column(step * TILE, part)
        for h in range(heads):
            r = k * heads + h
            picks[r * part : (r + 1) * part, :] = (place_lane == column + r).astype(F32).astype(BF16)

    wait_in(condition.at[pl.ds(0, groups - 1)], cond_sems.at[1])
    wait_in(arrived.at[pl.ds(1, shards - 1)], row_sems.at[1])

    def pass_on(k, index, block, target):
        copy = pltpu.make_async_remote_copy(
            src_ref=encoded.at[k, block],
            dst_ref=encoded.at[k, block],
            send_sem=enc_send.at[k, index],
            recv_sem=enc_recv.at[k, index],
            device_id=target,
            device_id_type=MESH,
        )
        copy.start()
        return copy

    over_x, to_sibling = [], []
    cond = condition[...].reshape(spans, span_len, enc_width)
    rows_in = arrived[...].reshape(shards * TILE, LANES)
    for k in range(spans):
        embedded = jnp.dot(
            picks[k * heads * part : (k + 1) * heads * part, :], rows_in, preferred_element_type=F32
        )
        embedded_bf16 = embedded.astype(BF16)
        scores = []
        for h in range(heads):
            scores.append(
                lax.dot_general(
                    embedded_bf16[h * part : (h + 1) * part],
                    cond[k, :, h * LANES : (h + 1) * LANES],
                    (((1,), (1,)), ((), ())),
                    preferred_element_type=F32,
                )
            )
        weights = softmax(jnp.concatenate(scores, axis=0) * (1.0 / math.sqrt(LANES)))
        for h in range(heads):
            added = jnp.dot(
                weights[h * part : (h + 1) * part],
                cond[k, :, h * LANES : (h + 1) * LANES],
                preferred_element_type=F32,
            )
            encoded[k, group, :, h * LANES : (h + 1) * LANES] = (
                embedded[h * part : (h + 1) * part] + added
            ).astype(BF16)
        over_x.append([pass_on(k, dx, group, group_peer(0, dx)) for dx in range(1, mps)])
        to_sibling.append([pass_on(k, mps, group, group_peer(1, 0))])

    def forward(k):
        for dx in range(1, mps):
            over_x[k][dx - 1].wait_recv()
            block = section * mps + lax.rem(mp + mps - dx, mps)
            to_sibling[k].append(pass_on(k, mps + dx, block, group_peer(1, 0)))

    def gathered(k):
        for copy in to_sibling[k]:
            copy.wait_recv()

    width = kv_weight.shape[1] // 2
    local_heads = width // HD
    row_count = groups * part

    def project(k):
        rows = encoded[k].reshape(row_count, enc_width)
        return jnp.dot(rows, kv_weight[...], preferred_element_type=F32).astype(BF16)

    def attend(k, key_value):
        scores = []
        for t in range(local_heads):
            scores.append(
                lax.dot_general(
                    queries[k * span_len : (k + 1) * span_len, t * HD : (t + 1) * HD],
                    key_value[:, t * HD : (t + 1) * HD],
                    (((1,), (1,)), ((), ())),
                    preferred_element_type=F32,
                )
            )
        scores = jnp.concatenate(scores, axis=0) * (1.0 / math.sqrt(HD))
        neighbour = lax.broadcasted_iota(jnp.int32, scores.shape, 1) // (row_count // sections)
        weights = softmax(jnp.where(neighbour.astype(F32) < kept[k], scores, -jnp.inf))
        for t in range(local_heads):
            out[k * span_len : (k + 1) * span_len, t * HD : (t + 1) * HD] = jnp.dot(
                weights[t * span_len : (t + 1) * span_len],
                key_value[:, width + t * HD : width + (t + 1) * HD],
                preferred_element_type=F32,
            ).astype(BF16)

    loads[4].wait()
    forward(0)
    gathered(0)
    for k in range(spans):
        key_value = project(k)
        if k + 1 < spans:
            forward(k + 1)
        attend(k, key_value)
        if k + 1 < spans:
            gathered(k + 1)

    wait_out(facts_far.at[pl.ds(0, shards - 1)], facts_sems.at[0])
    wait_out(answers_far.at[pl.ds(1, shards - 1)], row_sems.at[0])
    wait_out(partial_out.at[pl.ds(1, groups - 1)], part_sems.at[0])
    wait_out(condition.at[pl.ds(1, groups - 1)], cond_sems.at[0])
    for copy in sum(over_x + to_sibling, []):
        copy.wait_send()


def softmax(scores):
    high = jnp.max(scores, axis=1, keepdims=True)
    raised = jnp.exp(scores - high)
    return (raised / jnp.sum(raised, axis=1, keepdims=True)).astype(BF16)


def per_device(
    mesh_shape, span_states, queries, slot_span, neighbour_ids, neighbour_count, table, cond_weight, kv_weight
):
    shards, sections, mps = mesh_shape["seq"], mesh_shape["section"], mesh_shape["mp"]
    groups = sections * mps
    spans = slot_span.shape[0]
    part = neighbour_ids.shape[1] // groups
    tokens, width = queries.shape
    vocab, enc_width = table.shape
    pairs = 2 * width // LANES
    kv_rows = (
        kv_weight.reshape(enc_width, 2, width // LANES, LANES)
        .transpose(0, 2, 1, 3)
        .reshape(enc_width * pairs, LANES)
    )
    vmem = pl.BlockSpec(memory_space=pltpu.VMEM)
    hbm = pl.BlockSpec(memory_space=pltpu.HBM)
    rows_14 = spans * (enc_width // LANES)
    block_rows = tokens // groups
    dma = pltpu.SemaphoreType.DMA
    return pl.pallas_call(
        functools.partial(kernel, (shards, sections, mps, spans, part, tokens // spans)),
        out_shape=jax.ShapeDtypeStruct(queries.shape, queries.dtype),
        in_specs=[hbm] * 8,
        out_specs=vmem,
        scratch_shapes=[
            pltpu.SMEM(slot_span.shape, jnp.int32),
            pltpu.SMEM(neighbour_count.shape, jnp.int32),
            pltpu.VMEM(neighbour_ids.shape, jnp.int32),
            pltpu.VMEM(span_states.shape, BF16),
            pltpu.VMEM(queries.shape, BF16),
            pltpu.VMEM(table.shape, BF16),
            pltpu.VMEM(cond_weight.shape, BF16),
            pltpu.VMEM(kv_rows.shape, BF16),
            pltpu.VMEM((enc_width, 2 * width), BF16),
            pltpu.VMEM((enc_width // 8 * pairs, LANES), F32),
            pltpu.VMEM((shards, LANES), jnp.int32),
            pltpu.VMEM((shards, LANES), jnp.int32),
            pltpu.VMEM((shards * TILE, LANES), F32),
            pltpu.VMEM((shards, TILE, LANES), BF16),
            pltpu.VMEM((shards, TILE, LANES), BF16),
            pltpu.VMEM((shards, TILE, LANES), BF16),
            pltpu.VMEM((rows_14 * part, shards * TILE), BF16),
            pltpu.VMEM((groups, block_rows, enc_width), F32),
            pltpu.VMEM((groups, block_rows, enc_width), BF16),
            pltpu.VMEM((groups, block_rows, enc_width), BF16),
            pltpu.VMEM((groups, block_rows, enc_width), BF16),
            pltpu.VMEM((spans, groups, part, enc_width), BF16),
            dma((8,)),
            dma((3,)),
            dma((2,)),
            dma((2,)),
            dma((2,)),
            dma((spans, 2 * mps)),
            dma((spans, 2 * mps)),
        ],
        compiler_params=pltpu.CompilerParams(
            collective_id=0, has_side_effects=True, vmem_limit_bytes=60 * 1024 * 1024
        ),
    )(slot_span, neighbour_count, neighbour_ids, span_states, queries, table, cond_weight, kv_rows)


def solution(mesh):
    placed = (
        P("seq", ("section", "mp")),
        P("seq", ("section", "mp")),
        P("seq"),
        P("seq", None),
        P("seq"),
        P("seq", None),
        P(("section", "mp"), None),
        P(None, None, ("section", "mp")),
    )
    return jax.shard_map(
        functools.partial(per_device, dict(mesh.shape)),
        mesh=mesh,
        in_specs=placed,
        out_specs=P("seq", ("section", "mp")),
        check_vma=False,
    )
```

```python
import functools
import math

import jax
import jax.numpy as jnp
from jax import lax
from jax.experimental import pallas as pl
from jax.experimental.pallas import tpu as pltpu
from jax.sharding import PartitionSpec as P

HD = 128
LANES = 128
TILE = 16
RINGS = 4
BF16 = jnp.bfloat16
F32 = jnp.float32
MESH = pl.DeviceIdType.MESH


def to_column(row, rows):
    shape = (rows, row.shape[1])
    here = lax.broadcasted_iota(jnp.int32, shape, 0) == lax.broadcasted_iota(jnp.int32, shape, 1)
    return jnp.sum(jnp.where(here, row, 0.0), axis=1, keepdims=True)


def lane_sum(mask, values):
    return jnp.sum(jnp.where(mask, values, 0.0), axis=1, keepdims=True)


def kernel(
    sizes,
    slot_span_hbm,
    counts_hbm,
    ids_hbm,
    states_hbm,
    queries_hbm,
    table_hbm,
    cond_weight_hbm,
    kv_hbm,
    out,
    slot_span,
    counts,
    ids,
    states,
    queries,
    queries_other,
    table,
    cond_weight,
    kv_raw,
    kv_weight,
    kv_other,
    kv_f32,
    facts,
    asked_f32,
    answers,
    arrived,
    picks,
    partial,
    partial_out,
    partial_in,
    condition,
    encoded,
    reply,
    given,
    local_sems,
    facts_sems,
    row_sems,
    part_sems,
    cond_sems,
    enc_send,
    enc_recv,
    pair_send,
    pair_recv,
):
    shards, sections, mps, spans, part, span_len = sizes
    groups = sections * mps
    enc_width = table.shape[1]
    heads = enc_width // LANES
    vocab = table.shape[0]
    me = lax.axis_index("seq")
    section = lax.axis_index("section")
    mp = lax.axis_index("mp")
    group = section * mps + mp
    positions = sections * part

    loads = [
        pltpu.make_async_copy(src, dst, local_sems.at[n])
        for n, (src, dst) in enumerate(
            (
                (states_hbm, states),
                (cond_weight_hbm, cond_weight),
                (table_hbm, table),
                (kv_hbm, kv_raw),
                (queries_hbm, queries),
                (ids_hbm, ids),
                (slot_span_hbm, slot_span),
                (counts_hbm, counts),
            )
        )
    ]
    for n in (5, 6, 7, 3, 0, 1, 2, 4):
        loads[n].start()

    half = shards // 2
    rings = facts.shape[0]

    def seq_peer(d):
        return {"seq": lax.rem(me + d, shards)}

    def over_peers(low, high, act):
        def body(i, carry):
            act(half + (i + 1) // 2 * (1 - 2 * lax.rem(i, 2)))
            return carry

        lax.fori_loop(low, high, body, 0)

    def within(distance):
        return max(0, shards - 1 - 2 * distance)

    reach = [half * (c + 1) // rings for c in range(rings)]
    row_ends = [within(b) for b in [0] + reach]
    fact_ends = [shards - 1] + [within(b + 1) for b in reach]

    def wait_in(ref, sem):
        pltpu.make_async_remote_copy(
            src_ref=ref, dst_ref=ref, send_sem=sem, recv_sem=sem, device_id=seq_peer(1), device_id_type=MESH
        ).wait_recv()

    def wait_out(ref, sem):
        pltpu.make_async_remote_copy(
            src_ref=ref, dst_ref=ref, send_sem=sem, recv_sem=sem, device_id=seq_peer(1), device_id_type=MESH
        ).wait_send()

    def group_peer(ds, dx):
        return {"section": lax.rem(section + ds, sections), "mp": lax.rem(mp + dx, mps)}

    group_steps = [(ds, dx) for ds in range(sections) for dx in range(mps)][1:]

    barrier = pltpu.get_barrier_semaphore()
    facts[...] = jnp.full(facts.shape, -1, jnp.int32)
    over_peers(
        0, shards - 1, lambda d: pl.semaphore_signal(barrier, inc=1, device_id=seq_peer(d), device_id_type=MESH)
    )
    for ds, dx in group_steps:
        pl.semaphore_signal(barrier, inc=1, device_id=group_peer(ds, dx), device_id_type=MESH)

    lane = lax.broadcasted_iota(jnp.int32, (1, LANES), 1)
    for load in loads[5:]:
        load.wait()
    all_ids = ids[...]
    message = jnp.zeros((spans, LANES), jnp.int32)
    lanes_2 = lax.broadcasted_iota(jnp.int32, message.shape, 1)
    for g in range(sections):
        first = g * mps * part // LANES * LANES
        line = pltpu.roll(all_ids[:, first : first + LANES], lax.rem(2 * LANES + g * part - mp * part, LANES), 1)
        message = jnp.where((lanes_2 >= g * part) & (lanes_2 < (g + 1) * part), line, message)
    for k in range(spans):
        here = lax.broadcasted_iota(jnp.int32, message.shape, 0) == k
        message = jnp.where(here & (lanes_2 == positions), slot_span[k], message)
        message = jnp.where(here & (lanes_2 == positions + 1), counts[k], message)
    facts[0, 0:spans, :] = message

    loads[0].wait()
    loads[1].wait()
    product = jnp.dot(states[...], cond_weight[...], preferred_element_type=F32)
    block_rows = product.shape[0] // groups
    partial[...] = product.reshape(groups, block_rows, enc_width)
    partial_out[...] = product.astype(BF16).reshape(groups, block_rows, enc_width)

    loads[3].wait()
    pairs = kv_weight.shape[1] // LANES
    step_rows = kv_f32.shape[0] // pairs

    def split_pairs(step, carry):
        rows = pl.ds(pl.multiple_of(step * step_rows * pairs, TILE), step_rows * pairs)
        kv_f32[...] = kv_raw[rows, :].astype(F32)
        for t in range(pairs // 2):
            for j in range(2):
                column = (j * (pairs // 2) + t) * LANES
                kv_weight[pl.ds(pl.multiple_of(step * step_rows, TILE), step_rows), column : column + LANES] = (
                    kv_f32[pl.ds(t * 2 + j, step_rows, stride=pairs), :].astype(BF16)
                )
        return carry

    lax.fori_loop(0, kv_weight.shape[0] // step_rows, split_pairs, 0)
    asked_f32[...] = jnp.zeros_like(asked_f32)

    pl.semaphore_wait(barrier, shards - 1 + len(group_steps))

    def tell(ring):
        def act(d):
            pltpu.make_async_remote_copy(
                src_ref=facts.at[0, pl.ds(0, spans)],
                dst_ref=facts.at[ring, pl.ds((shards - d) * spans, spans)],
                send_sem=facts_sems.at[rings],
                recv_sem=facts_sems.at[ring],
                device_id=seq_peer(d),
                device_id_type=MESH,
            ).start()

        return act

    for ring in reversed(range(rings)):
        over_peers(fact_ends[ring + 1], fact_ends[ring], tell(ring))

    for ds, dx in group_steps:
        to = lax.rem(section + ds, sections) * mps + lax.rem(mp + dx, mps)
        back = ((sections - ds) % sections) * mps + (mps - dx) % mps
        pltpu.make_async_remote_copy(
            src_ref=partial_out.at[to],
            dst_ref=partial_in.at[back],
            send_sem=part_sems.at[0],
            recv_sem=part_sems.at[1],
            device_id=group_peer(ds, dx),
            device_id_type=MESH,
        ).start()

    def pair_copy(index, src, dst):
        copy = pltpu.make_async_remote_copy(
            src_ref=src,
            dst_ref=dst,
            send_sem=pair_send.at[index],
            recv_sem=pair_recv.at[index],
            device_id=group_peer(1, 0),
            device_id_type=MESH,
        )
        copy.start()
        return copy

    loads[4].wait()
    own_rows = pl.ds(pl.multiple_of(section * span_len, TILE), span_len)
    other_rows = pl.ds(pl.multiple_of((1 - section) * span_len, TILE), span_len)
    pair_copies = [
        pair_copy(0, queries.at[other_rows], queries_other),
        pair_copy(1, kv_weight, kv_other),
    ]

    wide = (shards, LANES)
    lanes = lax.broadcasted_iota(jnp.int32, wide, 1)
    rows_d = lax.broadcasted_iota(jnp.int32, wide, 0)
    span_row = (lax.rem(me + lax.rem(lane, shards), shards) * spans + lane // shards).astype(F32)
    span_row = jnp.where(lane < spans * shards, span_row, -2.0)
    vocab_lane = lax.broadcasted_iota(jnp.int32, (shards, vocab), 1).astype(F32)

    def look_up(told, ring):
        slots = jnp.where(section == 0, told[0], told[1]).astype(F32)
        slot_holds = lane_sum(lanes == positions, slots)
        wanted = span_row == slot_holds
        marks = []
        for g in range(sections):
            want_row = jnp.zeros((1, LANES), F32)
            for k in range(spans):
                local = told[k] - me * vocab
                inside = (local >= 0) & (local < vocab)
                want = lane_sum(inside & (lanes >= g * part) & (lanes < (g + 1) * part), (local + 1).astype(F32))
                want_row += jnp.sum(jnp.where(lanes == rows_d + k * shards, want, 0.0), axis=0, keepdims=True)
            request = lane_sum(wanted, want_row) - 1.0
            marks.append((vocab_lane == request).astype(F32).astype(BF16))
        rows_out = jnp.dot(jnp.concatenate(marks, axis=0), table[...], preferred_element_type=F32)
        for g in range(sections):
            for h in range(heads):
                asked_f32[pl.ds(g * heads + h, shards, stride=TILE), :] = rows_out[
                    g * shards : (g + 1) * shards, h * LANES : (h + 1) * LANES
                ]
        answers[ring] = asked_f32[...].astype(BF16).reshape(answers.shape[1:])

    def answer(ring):
        def act(d):
            pltpu.make_async_remote_copy(
                src_ref=answers.at[ring, d],
                dst_ref=arrived.at[shards - d],
                send_sem=row_sems.at[0],
                recv_sem=row_sems.at[1],
                device_id=seq_peer(d),
                device_id_type=MESH,
            ).start()

        return act

    def sum_condition():
        wait_in(partial_in.at[pl.ds(1, groups - 1)], part_sems.at[1])
        total = partial[group]
        for n in range(1, groups):
            total += partial_in[n].astype(F32)
        condition[mp] = total.astype(BF16)
        for dx in range(1, mps):
            pltpu.make_async_remote_copy(
                src_ref=condition.at[mp],
                dst_ref=condition.at[mp],
                send_sem=cond_sems.at[0],
                recv_sem=cond_sems.at[1],
                device_id=group_peer(0, dx),
                device_id_type=MESH,
            ).start()

    loads[2].wait()
    told = [jnp.full(wide, -1, jnp.int32)] * spans
    for ring in range(rings):
        heard = (fact_ends[ring] - fact_ends[ring + 1]) * spans
        wait_in(facts.at[ring, pl.ds(0, heard)], facts_sems.at[ring])
        told = [jnp.maximum(told[k], facts[ring, pl.ds(k, shards, stride=spans), :]) for k in range(spans)]
        if ring == 0:
            near = told
        look_up(told, ring)
        over_peers(row_ends[ring + 1], row_ends[ring], answer(ring))
        if ring == 0:
            arrived[0] = answers[0, 0]
            sum_condition()

    held = slot_span[section]
    span_at = lax.rem(me + rows_d[:, :1], shards) * spans
    chosen = jnp.zeros((1, LANES), F32)
    for home in range(spans):
        chosen += jnp.sum(jnp.where(span_at + home == held, near[home].astype(F32), 0.0), axis=0, keepdims=True)
    count = lane_sum(lane == positions + 1, chosen)
    owner = jnp.floor((chosen + 0.5) * (1.0 / vocab))
    step = owner - me.astype(F32)
    step = jnp.where(step < 0, step + shards, step)
    column = to_column(step * TILE, positions)
    column += (lax.broadcasted_iota(jnp.int32, column.shape, 0) // part * heads).astype(F32)
    place_lane = lax.broadcasted_iota(jnp.int32, (positions, shards * TILE), 1).astype(F32)
    for h in range(heads):
        picks[h * positions : (h + 1) * positions, :] = (place_lane == column + h).astype(F32).astype(BF16)

    wait_in(condition.at[pl.ds(0, mps - 1)], cond_sems.at[1])
    wait_in(arrived.at[pl.ds(1, shards - 1)], row_sems.at[1])

    embedded = jnp.dot(
        picks[...], arrived[...].reshape(shards * TILE, LANES), preferred_element_type=F32
    )
    embedded_bf16 = embedded.astype(BF16)
    cond = condition[...].reshape(span_len, enc_width)
    scores = []
    for h in range(heads):
        scores.append(
            lax.dot_general(
                embedded_bf16[h * positions : (h + 1) * positions],
                cond[:, h * LANES : (h + 1) * LANES],
                (((1,), (1,)), ((), ())),
                preferred_element_type=F32,
            )
        )
    weights = softmax(jnp.concatenate(scores, axis=0) * (1.0 / math.sqrt(LANES)))
    for h in range(heads):
        added = jnp.dot(
            weights[h * positions : (h + 1) * positions],
            cond[:, h * LANES : (h + 1) * LANES],
            preferred_element_type=F32,
        )
        rows = (embedded[h * positions : (h + 1) * positions] + added).astype(BF16)
        encoded[mp, :, :, h * LANES : (h + 1) * LANES] = rows.reshape(sections, part, LANES)

    over_x = []
    for g in range(sections):
        over_x.append([])
        for dx in range(1, mps):
            copy = pltpu.make_async_remote_copy(
                src_ref=encoded.at[mp, g],
                dst_ref=encoded.at[mp, g],
                send_sem=enc_send.at[g, dx],
                recv_sem=enc_recv.at[g, dx],
                device_id=group_peer(0, dx),
                device_id_type=MESH,
            )
            copy.start()
            over_x[g].append(copy)

    width = kv_weight.shape[1] // 2
    local_heads = width // HD
    row_count = mps * part

    def project(g, weight):
        rows = encoded[:, g].reshape(row_count, enc_width)
        return jnp.dot(rows, weight[...], preferred_element_type=F32).astype(BF16)

    def attend(query, key_value):
        scores = []
        for t in range(local_heads):
            scores.append(
                jnp.concatenate(
                    [
                        lax.dot_general(
                            query[:, t * HD : (t + 1) * HD],
                            block[:, t * HD : (t + 1) * HD],
                            (((1,), (1,)), ((), ())),
                            preferred_element_type=F32,
                        )
                        for block in key_value
                    ],
                    axis=1,
                )
            )
        scores = jnp.concatenate(scores, axis=0) * (1.0 / math.sqrt(HD))
        neighbour = lax.broadcasted_iota(jnp.int32, scores.shape, 1) // row_count
        weights = softmax(jnp.where(neighbour.astype(F32) < count, scores, -jnp.inf))
        done = []
        for t in range(local_heads):
            added = [
                jnp.dot(
                    weights[t * span_len : (t + 1) * span_len, n * row_count : (n + 1) * row_count],
                    block[:, width + t * HD : width + (t + 1) * HD],
                    preferred_element_type=F32,
                )
                for n, block in enumerate(key_value)
            ]
            done.append(functools.reduce(jnp.add, added).astype(BF16))
        return jnp.concatenate(done, axis=1)

    for copy in pair_copies:
        copy.wait_recv()
    theirs, ours = [], []
    for g in range(sections):
        for copy in over_x[g]:
            copy.wait_recv()
        theirs.append(project(g, kv_other))
        if g + 1 < sections:
            ours.append(project(g, kv_weight))
    reply[...] = attend(queries_other[...], theirs)
    pair_copies.append(pair_copy(2, reply, given))
    ours.append(project(sections - 1, kv_weight))
    out[own_rows, :] = attend(queries[own_rows, :], ours)

    wait_out(facts.at[0, pl.ds(0, (shards - 1) * spans)], facts_sems.at[rings])
    wait_out(answers.at[0, pl.ds(1, shards - 1)], row_sems.at[0])
    wait_out(partial_out.at[pl.ds(1, groups - 1)], part_sems.at[0])
    wait_out(condition.at[pl.ds(1, mps - 1)], cond_sems.at[0])
    for copy in sum(over_x, []) + pair_copies:
        copy.wait_send()
    pair_copies[-1].wait_recv()
    out[other_rows, :] = given[...]


def softmax(scores):
    high = jnp.max(scores, axis=1, keepdims=True)
    raised = jnp.exp(scores - high)
    return (raised / jnp.sum(raised, axis=1, keepdims=True)).astype(BF16)


def per_device(
    mesh_shape, span_states, queries, slot_span, neighbour_ids, neighbour_count, table, cond_weight, kv_weight
):
    shards, sections, mps = mesh_shape["seq"], mesh_shape["section"], mesh_shape["mp"]
    groups = sections * mps
    spans = slot_span.shape[0]
    part = neighbour_ids.shape[1] // groups
    tokens, width = queries.shape
    vocab, enc_width = table.shape
    pairs = 2 * width // LANES
    kv_rows = (
        kv_weight.reshape(enc_width, 2, width // LANES, LANES)
        .transpose(0, 2, 1, 3)
        .reshape(enc_width * pairs, LANES)
    )
    vmem = pl.BlockSpec(memory_space=pltpu.VMEM)
    hbm = pl.BlockSpec(memory_space=pltpu.HBM)
    rows_out = groups // mps * (enc_width // LANES)
    block_rows = tokens // groups
    span_len = tokens // spans
    dma = pltpu.SemaphoreType.DMA
    return pl.pallas_call(
        functools.partial(kernel, (shards, sections, mps, spans, part, span_len)),
        out_shape=jax.ShapeDtypeStruct(queries.shape, queries.dtype),
        in_specs=[hbm] * 8,
        out_specs=vmem,
        scratch_shapes=[
            pltpu.SMEM(slot_span.shape, jnp.int32),
            pltpu.SMEM(neighbour_count.shape, jnp.int32),
            pltpu.VMEM(neighbour_ids.shape, jnp.int32),
            pltpu.VMEM(span_states.shape, BF16),
            pltpu.VMEM(queries.shape, BF16),
            pltpu.VMEM((span_len, width), BF16),
            pltpu.VMEM(table.shape, BF16),
            pltpu.VMEM(cond_weight.shape, BF16),
            pltpu.VMEM(kv_rows.shape, BF16),
            pltpu.VMEM((enc_width, 2 * width), BF16),
            pltpu.VMEM((enc_width, 2 * width), BF16),
            pltpu.VMEM((enc_width // 8 * pairs, LANES), F32),
            pltpu.VMEM((RINGS, shards * spans, LANES), jnp.int32),
            pltpu.VMEM((shards * TILE, LANES), F32),
            pltpu.VMEM((RINGS, shards, TILE, LANES), BF16),
            pltpu.VMEM((shards, TILE, LANES), BF16),
            pltpu.VMEM((rows_out * part, shards * TILE), BF16),
            pltpu.VMEM((groups, block_rows, enc_width), F32),
            pltpu.VMEM((groups, block_rows, enc_width), BF16),
            pltpu.VMEM((groups, block_rows, enc_width), BF16),
            pltpu.VMEM((mps, block_rows, enc_width), BF16),
            pltpu.VMEM((mps, sections, part, enc_width), BF16),
            pltpu.VMEM((span_len, width), BF16),
            pltpu.VMEM((span_len, width), BF16),
            dma((8,)),
            dma((RINGS + 1,)),
            dma((2,)),
            dma((2,)),
            dma((2,)),
            dma((sections, mps)),
            dma((sections, mps)),
            dma((3,)),
            dma((3,)),
        ],
        compiler_params=pltpu.CompilerParams(
            collective_id=0, has_side_effects=True, vmem_limit_bytes=60 * 1024 * 1024
        ),
    )(slot_span, neighbour_count, neighbour_ids, span_states, queries, table, cond_weight, kv_rows)


def solution(mesh):
    placed = (
        P("seq", ("section", "mp")),
        P("seq", ("section", "mp")),
        P("seq"),
        P("seq", None),
        P("seq"),
        P("seq", None),
        P(("section", "mp"), None),
        P(None, None, ("section", "mp")),
    )
    return jax.shard_map(
        functools.partial(per_device, dict(mesh.shape)),
        mesh=mesh,
        in_specs=placed,
        out_specs=P("seq", ("section", "mp")),
        check_vma=False,
    )
```

```python
import functools
import math

import jax
import jax.numpy as jnp
from jax import lax
from jax.experimental import pallas as pl
from jax.experimental.pallas import tpu as pltpu
from jax.sharding import PartitionSpec as P

HD = 128
LANES = 128
TILE = 16
RINGS = 2
BF16 = jnp.bfloat16
F32 = jnp.float32
MESH = pl.DeviceIdType.MESH


def to_column(row, rows):
    shape = (rows, row.shape[1])
    here = lax.broadcasted_iota(jnp.int32, shape, 0) == lax.broadcasted_iota(jnp.int32, shape, 1)
    return jnp.sum(jnp.where(here, row, 0.0), axis=1, keepdims=True)


def lane_sum(mask, values):
    return jnp.sum(jnp.where(mask, values, 0.0), axis=1, keepdims=True)


def kernel(
    sizes,
    slot_span_hbm,
    counts_hbm,
    ids_hbm,
    states_hbm,
    queries_hbm,
    table_hbm,
    cond_weight_hbm,
    kv_hbm,
    out,
    slot_span,
    counts,
    ids,
    states,
    queries,
    queries_other,
    table,
    cond_weight,
    kv_raw,
    kv_weight,
    kv_other,
    kv_f32,
    facts,
    asked_f32,
    answers,
    arrived,
    picks,
    partial,
    partial_out,
    partial_in,
    condition,
    encoded,
    reply,
    given,
    local_sems,
    facts_sems,
    row_sems,
    part_sems,
    cond_sems,
    enc_send,
    enc_recv,
    pair_send,
    pair_recv,
):
    shards, sections, mps, spans, part, span_len = sizes
    groups = sections * mps
    enc_width = table.shape[1]
    heads = enc_width // LANES
    vocab = table.shape[0]
    me = lax.axis_index("seq")
    section = lax.axis_index("section")
    mp = lax.axis_index("mp")
    group = section * mps + mp
    positions = sections * part

    loads = [
        pltpu.make_async_copy(src, dst, local_sems.at[n])
        for n, (src, dst) in enumerate(
            (
                (states_hbm, states),
                (cond_weight_hbm, cond_weight),
                (table_hbm, table),
                (kv_hbm, kv_raw),
                (queries_hbm, queries),
                (ids_hbm, ids),
                (slot_span_hbm, slot_span),
                (counts_hbm, counts),
            )
        )
    ]
    half = shards // 2
    rings = facts.shape[0]

    def seq_peer(d):
        return {"seq": lax.rem(me + d, shards)}

    def over_peers(low, high, act):
        def body(i, carry):
            act(half + (i + 1) // 2 * (1 - 2 * lax.rem(i, 2)))
            return carry

        lax.fori_loop(low, high, body, 0)

    ring_width = shards // rings
    fact_counts = [ring_width + 2] + [ring_width] * (rings - 2) + [ring_width - 2] if rings > 1 else [shards]
    fact_ring = jnp.where(me == shards - 1, 0, jnp.maximum(me - 1, 0) // ring_width)
    own_facts = pl.ds(me * spans, spans)

    def wait_in(ref, sem):
        pltpu.make_async_remote_copy(
            src_ref=ref, dst_ref=ref, send_sem=sem, recv_sem=sem, device_id=seq_peer(1), device_id_type=MESH
        ).wait_recv()

    def wait_out(ref, sem):
        pltpu.make_async_remote_copy(
            src_ref=ref, dst_ref=ref, send_sem=sem, recv_sem=sem, device_id=seq_peer(1), device_id_type=MESH
        ).wait_send()

    def group_peer(ds, dx):
        return {"section": lax.rem(section + ds, sections), "mp": lax.rem(mp + dx, mps)}

    group_steps = [(ds, dx) for ds in range(sections) for dx in range(mps)][1:]

    barrier = pltpu.get_barrier_semaphore()
    facts[...] = jnp.full(facts.shape, -1, jnp.int32)
    over_peers(
        0, shards - 1, lambda d: pl.semaphore_signal(barrier, inc=1, device_id=seq_peer(d), device_id_type=MESH)
    )
    for ds, dx in group_steps:
        pl.semaphore_signal(barrier, inc=1, device_id=group_peer(ds, dx), device_id_type=MESH)

    for n in (5, 6, 7, 3, 0, 1, 2, 4):
        loads[n].start()

    lane = lax.broadcasted_iota(jnp.int32, (1, LANES), 1)
    for load in loads[5:]:
        load.wait()
    all_ids = ids[...]
    message = jnp.zeros((spans, LANES), jnp.int32)
    lanes_2 = lax.broadcasted_iota(jnp.int32, message.shape, 1)
    for g in range(sections):
        first = g * mps * part // LANES * LANES
        line = pltpu.roll(all_ids[:, first : first + LANES], lax.rem(2 * LANES + g * part - mp * part, LANES), 1)
        message = jnp.where((lanes_2 >= g * part) & (lanes_2 < (g + 1) * part), line, message)
    for k in range(spans):
        here = lax.broadcasted_iota(jnp.int32, message.shape, 0) == k
        message = jnp.where(here & (lanes_2 == positions), slot_span[k], message)
        message = jnp.where(here & (lanes_2 == positions + 1), counts[k], message)
    facts[fact_ring, own_facts, :] = message

    loads[0].wait()
    loads[1].wait()
    product = jnp.dot(states[...], cond_weight[...], preferred_element_type=F32)
    block_rows = product.shape[0] // groups
    partial[...] = product.reshape(groups, block_rows, enc_width)
    partial_out[...] = product.astype(BF16).reshape(groups, block_rows, enc_width)

    loads[3].wait()
    pairs = kv_weight.shape[1] // LANES
    step_rows = kv_f32.shape[0] // pairs

    def split_pairs(step, carry):
        rows = pl.ds(pl.multiple_of(step * step_rows * pairs, TILE), step_rows * pairs)
        kv_f32[...] = kv_raw[rows, :].astype(F32)
        for t in range(pairs // 2):
            for j in range(2):
                column = (j * (pairs // 2) + t) * LANES
                kv_weight[pl.ds(pl.multiple_of(step * step_rows, TILE), step_rows), column : column + LANES] = (
                    kv_f32[pl.ds(t * 2 + j, step_rows, stride=pairs), :].astype(BF16)
                )
        return carry

    lax.fori_loop(0, kv_weight.shape[0] // step_rows, split_pairs, 0)
    asked_f32[...] = jnp.zeros_like(asked_f32)

    pl.semaphore_wait(barrier, shards - 1 + len(group_steps))

    def tell(d):
        pltpu.make_async_remote_copy(
            src_ref=facts.at[fact_ring, own_facts],
            dst_ref=facts.at[fact_ring, own_facts],
            send_sem=facts_sems.at[rings],
            recv_sem=facts_sems.at[fact_ring],
            device_id=seq_peer(d),
            device_id_type=MESH,
        ).start()

    over_peers(0, shards - 1, tell)

    for ds, dx in group_steps:
        to = lax.rem(section + ds, sections) * mps + lax.rem(mp + dx, mps)
        back = ((sections - ds) % sections) * mps + (mps - dx) % mps
        pltpu.make_async_remote_copy(
            src_ref=partial_out.at[to],
            dst_ref=partial_in.at[back],
            send_sem=part_sems.at[0],
            recv_sem=part_sems.at[1],
            device_id=group_peer(ds, dx),
            device_id_type=MESH,
        ).start()

    def pair_copy(index, src, dst):
        copy = pltpu.make_async_remote_copy(
            src_ref=src,
            dst_ref=dst,
            send_sem=pair_send.at[index],
            recv_sem=pair_recv.at[index],
            device_id=group_peer(1, 0),
            device_id_type=MESH,
        )
        copy.start()
        return copy

    loads[4].wait()
    own_rows = pl.ds(pl.multiple_of(section * span_len, TILE), span_len)
    other_rows = pl.ds(pl.multiple_of((1 - section) * span_len, TILE), span_len)
    pair_copies = [
        pair_copy(0, queries.at[other_rows], queries_other),
        pair_copy(1, kv_weight, kv_other),
    ]

    wide = (shards, LANES)
    lanes = lax.broadcasted_iota(jnp.int32, wide, 1)
    rows_j = lax.broadcasted_iota(jnp.int32, wide, 0)
    span_row = (lax.rem(lane, shards) * spans + lane // shards).astype(F32)
    span_row = jnp.where(lane < spans * shards, span_row, -2.0)
    vocab_lane = lax.broadcasted_iota(jnp.int32, (ring_width, vocab), 1).astype(F32)

    def look_up(told, ring):
        slots = jnp.where(section == 0, told[0], told[1]).astype(F32)
        slots = slots[ring * ring_width : (ring + 1) * ring_width]
        wanted = span_row == lane_sum(lanes[:ring_width] == positions, slots)
        marks = []
        for g in range(sections):
            want_row = jnp.zeros((1, LANES), F32)
            for k in range(spans):
                local = told[k] - me * vocab
                inside = (local >= 0) & (local < vocab)
                want = lane_sum(inside & (lanes >= g * part) & (lanes < (g + 1) * part), (local + 1).astype(F32))
                want_row += jnp.sum(jnp.where(lanes == rows_j + k * shards, want, 0.0), axis=0, keepdims=True)
            request = lane_sum(wanted, want_row) - 1.0
            marks.append((vocab_lane == request).astype(F32).astype(BF16))
        rows_out = jnp.dot(jnp.concatenate(marks, axis=0), table[...], preferred_element_type=F32)
        for g in range(sections):
            for h in range(heads):
                asked_f32[pl.ds(g * heads + h, ring_width, stride=TILE), :] = rows_out[
                    g * ring_width : (g + 1) * ring_width, h * LANES : (h + 1) * LANES
                ]
        answers[ring] = asked_f32[...].astype(BF16).reshape(answers.shape[1:])

    def answer(ring):
        def act(n, carry):
            to = ring * ring_width + n

            @pl.when(to != me)
            def _():
                pltpu.make_async_remote_copy(
                    src_ref=answers.at[ring, n],
                    dst_ref=arrived.at[me],
                    send_sem=row_sems.at[0],
                    recv_sem=row_sems.at[1],
                    device_id={"seq": to},
                    device_id_type=MESH,
                ).start()

            return carry

        lax.fori_loop(0, ring_width, act, 0)

    def sum_condition():
        wait_in(partial_in.at[pl.ds(1, groups - 1)], part_sems.at[1])
        total = partial[group]
        for n in range(1, groups):
            total += partial_in[n].astype(F32)
        condition[mp] = total.astype(BF16)
        for dx in range(1, mps):
            pltpu.make_async_remote_copy(
                src_ref=condition.at[mp],
                dst_ref=condition.at[mp],
                send_sem=cond_sems.at[0],
                recv_sem=cond_sems.at[1],
                device_id=group_peer(0, dx),
                device_id_type=MESH,
            ).start()

    loads[2].wait()
    told = [jnp.full(wide, -1, jnp.int32)] * spans
    for ring in range(rings):
        heard = facts.at[ring, pl.ds(0, fact_counts[ring] * spans)]
        heard_others = facts.at[ring, pl.ds(0, (fact_counts[ring] - 1) * spans)]

        @pl.when(fact_ring == ring)
        def _():
            wait_in(heard_others, facts_sems.at[ring])

        @pl.when(fact_ring != ring)
        def _():
            wait_in(heard, facts_sems.at[ring])

        told = [jnp.maximum(told[k], facts[ring, pl.ds(k, shards, stride=spans), :]) for k in range(spans)]
        look_up(told, ring)
        answer(ring)
    arrived[me] = answers[me // ring_width, lax.rem(me, ring_width)]
    sum_condition()

    held = slot_span[section]
    span_at = rows_j[:, :1] * spans
    chosen = jnp.zeros((1, LANES), F32)
    for home in range(spans):
        chosen += jnp.sum(jnp.where(span_at + home == held, told[home].astype(F32), 0.0), axis=0, keepdims=True)
    count = lane_sum(lane == positions + 1, chosen)
    owner = jnp.floor((chosen + 0.5) * (1.0 / vocab))
    column = to_column(owner * TILE, positions)
    column += (lax.broadcasted_iota(jnp.int32, column.shape, 0) // part * heads).astype(F32)
    place_lane = lax.broadcasted_iota(jnp.int32, (positions, shards * TILE), 1).astype(F32)
    for h in range(heads):
        picks[h * positions : (h + 1) * positions, :] = (place_lane == column + h).astype(F32).astype(BF16)

    wait_in(condition.at[pl.ds(0, mps - 1)], cond_sems.at[1])
    wait_in(arrived.at[pl.ds(1, shards - 1)], row_sems.at[1])

    embedded = jnp.dot(
        picks[...], arrived[...].reshape(shards * TILE, LANES), preferred_element_type=F32
    )
    embedded_bf16 = embedded.astype(BF16)
    cond = condition[...].reshape(span_len, enc_width)
    scores = []
    for h in range(heads):
        scores.append(
            lax.dot_general(
                embedded_bf16[h * positions : (h + 1) * positions],
                cond[:, h * LANES : (h + 1) * LANES],
                (((1,), (1,)), ((), ())),
                preferred_element_type=F32,
            )
        )
    weights = softmax(jnp.concatenate(scores, axis=0) * (1.0 / math.sqrt(LANES)))
    for h in range(heads):
        added = jnp.dot(
            weights[h * positions : (h + 1) * positions],
            cond[:, h * LANES : (h + 1) * LANES],
            preferred_element_type=F32,
        )
        rows = (embedded[h * positions : (h + 1) * positions] + added).astype(BF16)
        encoded[mp, :, :, h * LANES : (h + 1) * LANES] = rows.reshape(sections, part, LANES)

    over_x = []
    for g in range(sections):
        over_x.append([])
        for dx in range(1, mps):
            copy = pltpu.make_async_remote_copy(
                src_ref=encoded.at[mp, g],
                dst_ref=encoded.at[mp, g],
                send_sem=enc_send.at[g, dx],
                recv_sem=enc_recv.at[g, dx],
                device_id=group_peer(0, dx),
                device_id_type=MESH,
            )
            copy.start()
            over_x[g].append(copy)

    width = kv_weight.shape[1] // 2
    local_heads = width // HD
    row_count = mps * part

    def project(g, weight):
        rows = encoded[:, g].reshape(row_count, enc_width)
        return jnp.dot(rows, weight[...], preferred_element_type=F32).astype(BF16)

    def attend(query, key_value):
        scores = []
        for t in range(local_heads):
            scores.append(
                jnp.concatenate(
                    [
                        lax.dot_general(
                            query[:, t * HD : (t + 1) * HD],
                            block[:, t * HD : (t + 1) * HD],
                            (((1,), (1,)), ((), ())),
                            preferred_element_type=F32,
                        )
                        for block in key_value
                    ],
                    axis=1,
                )
            )
        scores = jnp.concatenate(scores, axis=0) * (1.0 / math.sqrt(HD))
        neighbour = lax.broadcasted_iota(jnp.int32, scores.shape, 1) // row_count
        weights = softmax(jnp.where(neighbour.astype(F32) < count, scores, -jnp.inf))
        done = []
        for t in range(local_heads):
            added = [
                jnp.dot(
                    weights[t * span_len : (t + 1) * span_len, n * row_count : (n + 1) * row_count],
                    block[:, width + t * HD : width + (t + 1) * HD],
                    preferred_element_type=F32,
                )
                for n, block in enumerate(key_value)
            ]
            done.append(functools.reduce(jnp.add, added).astype(BF16))
        return jnp.concatenate(done, axis=1)

    for copy in pair_copies:
        copy.wait_recv()
    theirs, ours = [], []
    for g in range(sections):
        for copy in over_x[g]:
            copy.wait_recv()
        theirs.append(project(g, kv_other))
        if g + 1 < sections:
            ours.append(project(g, kv_weight))
    reply[...] = attend(queries_other[...], theirs)
    pair_copies.append(pair_copy(2, reply, given))
    ours.append(project(sections - 1, kv_weight))
    out[own_rows, :] = attend(queries[own_rows, :], ours)

    wait_out(facts.at[0, pl.ds(0, (shards - 1) * spans)], facts_sems.at[rings])
    wait_out(arrived.at[pl.ds(1, shards - 1)], row_sems.at[0])
    wait_out(partial_out.at[pl.ds(1, groups - 1)], part_sems.at[0])
    wait_out(condition.at[pl.ds(1, mps - 1)], cond_sems.at[0])
    for copy in sum(over_x, []) + pair_copies:
        copy.wait_send()
    pair_copies[-1].wait_recv()
    out[other_rows, :] = given[...]


def softmax(scores):
    high = jnp.max(scores, axis=1, keepdims=True)
    raised = jnp.exp(scores - high)
    return (raised / jnp.sum(raised, axis=1, keepdims=True)).astype(BF16)


def per_device(
    mesh_shape, span_states, queries, slot_span, neighbour_ids, neighbour_count, table, cond_weight, kv_weight
):
    shards, sections, mps = mesh_shape["seq"], mesh_shape["section"], mesh_shape["mp"]
    groups = sections * mps
    spans = slot_span.shape[0]
    part = neighbour_ids.shape[1] // groups
    tokens, width = queries.shape
    vocab, enc_width = table.shape
    pairs = 2 * width // LANES
    kv_rows = (
        kv_weight.reshape(enc_width, 2, width // LANES, LANES)
        .transpose(0, 2, 1, 3)
        .reshape(enc_width * pairs, LANES)
    )
    vmem = pl.BlockSpec(memory_space=pltpu.VMEM)
    hbm = pl.BlockSpec(memory_space=pltpu.HBM)
    rows_out = groups // mps * (enc_width // LANES)
    block_rows = tokens // groups
    span_len = tokens // spans
    dma = pltpu.SemaphoreType.DMA
    return pl.pallas_call(
        functools.partial(kernel, (shards, sections, mps, spans, part, span_len)),
        out_shape=jax.ShapeDtypeStruct(queries.shape, queries.dtype),
        in_specs=[hbm] * 8,
        out_specs=vmem,
        scratch_shapes=[
            pltpu.SMEM(slot_span.shape, jnp.int32),
            pltpu.SMEM(neighbour_count.shape, jnp.int32),
            pltpu.VMEM(neighbour_ids.shape, jnp.int32),
            pltpu.VMEM(span_states.shape, BF16),
            pltpu.VMEM(queries.shape, BF16),
            pltpu.VMEM((span_len, width), BF16),
            pltpu.VMEM(table.shape, BF16),
            pltpu.VMEM(cond_weight.shape, BF16),
            pltpu.VMEM(kv_rows.shape, BF16),
            pltpu.VMEM((enc_width, 2 * width), BF16),
            pltpu.VMEM((enc_width, 2 * width), BF16),
            pltpu.VMEM((enc_width // 8 * pairs, LANES), F32),
            pltpu.VMEM((RINGS, shards * spans, LANES), jnp.int32),
            pltpu.VMEM((shards // RINGS * TILE, LANES), F32),
            pltpu.VMEM((RINGS, shards // RINGS, TILE, LANES), BF16),
            pltpu.VMEM((shards, TILE, LANES), BF16),
            pltpu.VMEM((rows_out * part, shards * TILE), BF16),
            pltpu.VMEM((groups, block_rows, enc_width), F32),
            pltpu.VMEM((groups, block_rows, enc_width), BF16),
            pltpu.VMEM((groups, block_rows, enc_width), BF16),
            pltpu.VMEM((mps, block_rows, enc_width), BF16),
            pltpu.VMEM((mps, sections, part, enc_width), BF16),
            pltpu.VMEM((span_len, width), BF16),
            pltpu.VMEM((span_len, width), BF16),
            dma((8,)),
            dma((RINGS + 1,)),
            dma((2,)),
            dma((2,)),
            dma((2,)),
            dma((sections, mps)),
            dma((sections, mps)),
            dma((3,)),
            dma((3,)),
        ],
        compiler_params=pltpu.CompilerParams(
            collective_id=0, has_side_effects=True, vmem_limit_bytes=60 * 1024 * 1024
        ),
    )(slot_span, neighbour_count, neighbour_ids, span_states, queries, table, cond_weight, kv_rows)


def solution(mesh):
    placed = (
        P("seq", ("section", "mp")),
        P("seq", ("section", "mp")),
        P("seq"),
        P("seq", None),
        P("seq"),
        P("seq", None),
        P(("section", "mp"), None),
        P(None, None, ("section", "mp")),
    )
    return jax.shard_map(
        functools.partial(per_device, dict(mesh.shape)),
        mesh=mesh,
        in_specs=placed,
        out_specs=P("seq", ("section", "mp")),
        check_vma=False,
    )
```

```python
import functools
import math

import jax
import jax.numpy as jnp
from jax import lax
from jax.experimental import pallas as pl
from jax.experimental.pallas import tpu as pltpu
from jax.sharding import PartitionSpec as P

HD = 128
LANES = 128
TILE = 16
RINGS = 4
BF16 = jnp.bfloat16
F32 = jnp.float32
MESH = pl.DeviceIdType.MESH


def to_column(row, rows):
    shape = (rows, row.shape[1])
    here = lax.broadcasted_iota(jnp.int32, shape, 0) == lax.broadcasted_iota(jnp.int32, shape, 1)
    return jnp.sum(jnp.where(here, row, 0.0), axis=1, keepdims=True)


def lane_sum(mask, values):
    return jnp.sum(jnp.where(mask, values, 0.0), axis=1, keepdims=True)


def kernel(
    sizes,
    own_info,
    states_hbm,
    queries_hbm,
    table_hbm,
    cond_weight_hbm,
    kv_hbm,
    out,
    states,
    queries,
    queries_other,
    table,
    cond_weight,
    kv_raw,
    kv_weight,
    kv_other,
    kv_f32,
    facts,
    asked_f32,
    answers,
    arrived,
    picks,
    partial,
    partial_out,
    partial_in,
    condition,
    encoded,
    reply,
    given,
    local_sems,
    facts_sems,
    row_sems,
    part_sems,
    cond_sems,
    enc_send,
    enc_recv,
    pair_send,
    pair_recv,
):
    shards, sections, mps, spans, part, span_len = sizes
    groups = sections * mps
    enc_width = table.shape[1]
    heads = enc_width // LANES
    vocab = table.shape[0]
    me = lax.axis_index("seq")
    section = lax.axis_index("section")
    mp = lax.axis_index("mp")
    group = section * mps + mp
    positions = sections * part

    loads = [
        pltpu.make_async_copy(src, dst, local_sems.at[n])
        for n, (src, dst) in enumerate(
            (
                (states_hbm, states),
                (cond_weight_hbm, cond_weight),
                (table_hbm, table),
                (kv_hbm, kv_raw),
                (queries_hbm, queries),
            )
        )
    ]
    half = shards // 2
    rings = facts.shape[0]

    def seq_peer(d):
        return {"seq": lax.rem(me + d, shards)}

    def over_peers(low, high, act):
        def body(i, carry):
            act(half + (i + 1) // 2 * (1 - 2 * lax.rem(i, 2)))
            return carry

        lax.fori_loop(low, high, body, 0)

    ring_width = shards // rings
    fact_counts = [ring_width + 2] + [ring_width] * (rings - 2) + [ring_width - 2] if rings > 1 else [shards]
    fact_ring = jnp.where(me == shards - 1, 0, jnp.maximum(me - 1, 0) // ring_width)
    own_facts = pl.ds(me * spans, spans)

    def wait_in(ref, sem):
        pltpu.make_async_remote_copy(
            src_ref=ref, dst_ref=ref, send_sem=sem, recv_sem=sem, device_id=seq_peer(1), device_id_type=MESH
        ).wait_recv()

    def wait_out(ref, sem):
        pltpu.make_async_remote_copy(
            src_ref=ref, dst_ref=ref, send_sem=sem, recv_sem=sem, device_id=seq_peer(1), device_id_type=MESH
        ).wait_send()

    def group_peer(ds, dx):
        return {"section": lax.rem(section + ds, sections), "mp": lax.rem(mp + dx, mps)}

    group_steps = [(ds, dx) for ds in range(sections) for dx in range(mps)][1:]

    barrier = pltpu.get_barrier_semaphore()
    facts[...] = jnp.full(facts.shape, -1, jnp.int32)
    over_peers(
        0, shards - 1, lambda d: pl.semaphore_signal(barrier, inc=1, device_id=seq_peer(d), device_id_type=MESH)
    )
    for ds, dx in group_steps:
        pl.semaphore_signal(barrier, inc=1, device_id=group_peer(ds, dx), device_id_type=MESH)

    for n in (3, 0, 1, 2, 4):
        loads[n].start()

    lane = lax.broadcasted_iota(jnp.int32, (1, LANES), 1)
    all_ids = own_info[0:spans, :]
    own_line = own_info[spans : spans + 1, :]
    message = jnp.zeros((spans, LANES), jnp.int32)
    lanes_2 = lax.broadcasted_iota(jnp.int32, message.shape, 1)
    for g in range(sections):
        first = g * mps * part // LANES * LANES
        line = pltpu.roll(all_ids[:, first : first + LANES], lax.rem(2 * LANES + g * part - mp * part, LANES), 1)
        message = jnp.where((lanes_2 >= g * part) & (lanes_2 < (g + 1) * part), line, message)
    for k in range(spans):
        here = lax.broadcasted_iota(jnp.int32, message.shape, 0) == k
        message = jnp.where(here & (lanes_2 == positions), own_line[:, k : k + 1], message)
        message = jnp.where(here & (lanes_2 == positions + 1), own_line[:, spans + k : spans + k + 1], message)
    facts[fact_ring, own_facts, :] = message

    loads[0].wait()
    loads[1].wait()
    product = jnp.dot(states[...], cond_weight[...], preferred_element_type=F32)
    block_rows = product.shape[0] // groups
    partial[...] = product.reshape(groups, block_rows, enc_width)
    partial_out[...] = product.astype(BF16).reshape(groups, block_rows, enc_width)

    loads[3].wait()
    pairs = kv_weight.shape[1] // LANES
    step_rows = kv_f32.shape[0] // pairs

    def split_pairs(step, carry):
        rows = pl.ds(pl.multiple_of(step * step_rows * pairs, TILE), step_rows * pairs)
        kv_f32[...] = kv_raw[rows, :].astype(F32)
        for t in range(pairs // 2):
            for j in range(2):
                column = (j * (pairs // 2) + t) * LANES
                kv_weight[pl.ds(pl.multiple_of(step * step_rows, TILE), step_rows), column : column + LANES] = (
                    kv_f32[pl.ds(t * 2 + j, step_rows, stride=pairs), :].astype(BF16)
                )
        return carry

    lax.fori_loop(0, kv_weight.shape[0] // step_rows, split_pairs, 0)
    asked_f32[...] = jnp.zeros_like(asked_f32)

    pl.semaphore_wait(barrier, shards - 1 + len(group_steps))

    def tell(d):
        pltpu.make_async_remote_copy(
            src_ref=facts.at[fact_ring, own_facts],
            dst_ref=facts.at[fact_ring, own_facts],
            send_sem=facts_sems.at[rings],
            recv_sem=facts_sems.at[fact_ring],
            device_id=seq_peer(d),
            device_id_type=MESH,
        ).start()

    over_peers(0, shards - 1, tell)

    for ds, dx in group_steps:
        to = lax.rem(section + ds, sections) * mps + lax.rem(mp + dx, mps)
        back = ((sections - ds) % sections) * mps + (mps - dx) % mps
        pltpu.make_async_remote_copy(
            src_ref=partial_out.at[to],
            dst_ref=partial_in.at[back],
            send_sem=part_sems.at[0],
            recv_sem=part_sems.at[1],
            device_id=group_peer(ds, dx),
            device_id_type=MESH,
        ).start()

    def pair_copy(index, src, dst):
        copy = pltpu.make_async_remote_copy(
            src_ref=src,
            dst_ref=dst,
            send_sem=pair_send.at[index],
            recv_sem=pair_recv.at[index],
            device_id=group_peer(1, 0),
            device_id_type=MESH,
        )
        copy.start()
        return copy

    loads[4].wait()
    own_rows = pl.ds(pl.multiple_of(section * span_len, TILE), span_len)
    other_rows = pl.ds(pl.multiple_of((1 - section) * span_len, TILE), span_len)
    pair_copies = [
        pair_copy(0, queries.at[other_rows], queries_other),
        pair_copy(1, kv_weight, kv_other),
    ]

    wide = (shards, LANES)
    lanes = lax.broadcasted_iota(jnp.int32, wide, 1)
    rows_j = lax.broadcasted_iota(jnp.int32, wide, 0)
    span_row = (lax.rem(lane, shards) * spans + lane // shards).astype(F32)
    span_row = jnp.where(lane < spans * shards, span_row, -2.0)
    vocab_lane = lax.broadcasted_iota(jnp.int32, (ring_width, vocab), 1).astype(F32)

    def look_up(told, ring):
        slots = jnp.where(section == 0, told[0], told[1]).astype(F32)
        slots = slots[ring * ring_width : (ring + 1) * ring_width]
        wanted = span_row == lane_sum(lanes[:ring_width] == positions, slots)
        marks = []
        for g in range(sections):
            want_row = jnp.zeros((1, LANES), F32)
            for k in range(spans):
                local = told[k] - me * vocab
                inside = (local >= 0) & (local < vocab)
                want = lane_sum(inside & (lanes >= g * part) & (lanes < (g + 1) * part), (local + 1).astype(F32))
                want_row += jnp.sum(jnp.where(lanes == rows_j + k * shards, want, 0.0), axis=0, keepdims=True)
            request = lane_sum(wanted, want_row) - 1.0
            marks.append((vocab_lane == request).astype(F32).astype(BF16))
        rows_out = jnp.dot(jnp.concatenate(marks, axis=0), table[...], preferred_element_type=F32)
        for g in range(sections):
            for h in range(heads):
                asked_f32[pl.ds(g * heads + h, ring_width, stride=TILE), :] = rows_out[
                    g * ring_width : (g + 1) * ring_width, h * LANES : (h + 1) * LANES
                ]
        answers[ring] = asked_f32[...].astype(BF16).reshape(answers.shape[1:])

    def answer(ring):
        def act(n, carry):
            to = ring * ring_width + n

            @pl.when(to != me)
            def _():
                pltpu.make_async_remote_copy(
                    src_ref=answers.at[ring, n],
                    dst_ref=arrived.at[me],
                    send_sem=row_sems.at[0],
                    recv_sem=row_sems.at[1],
                    device_id={"seq": to},
                    device_id_type=MESH,
                ).start()

            return carry

        lax.fori_loop(0, ring_width, act, 0)

    def sum_condition():
        wait_in(partial_in.at[pl.ds(1, groups - 1)], part_sems.at[1])
        total = partial[group]
        for n in range(1, groups):
            total += partial_in[n].astype(F32)
        condition[mp] = total.astype(BF16)
        for dx in range(1, mps):
            pltpu.make_async_remote_copy(
                src_ref=condition.at[mp],
                dst_ref=condition.at[mp],
                send_sem=cond_sems.at[0],
                recv_sem=cond_sems.at[1],
                device_id=group_peer(0, dx),
                device_id_type=MESH,
            ).start()

    loads[2].wait()
    told = [jnp.full(wide, -1, jnp.int32)] * spans
    for ring in range(rings):
        heard = facts.at[ring, pl.ds(0, fact_counts[ring] * spans)]
        heard_others = facts.at[ring, pl.ds(0, (fact_counts[ring] - 1) * spans)]

        @pl.when(fact_ring == ring)
        def _():
            wait_in(heard_others, facts_sems.at[ring])

        @pl.when(fact_ring != ring)
        def _():
            wait_in(heard, facts_sems.at[ring])

        told = [jnp.maximum(told[k], facts[ring, pl.ds(k, shards, stride=spans), :]) for k in range(spans)]
        look_up(told, ring)
        answer(ring)
    arrived[me] = answers[me // ring_width, lax.rem(me, ring_width)]
    sum_condition()

    held = jnp.where(section == 0, own_line[:, 0:1], own_line[:, 1:2])
    span_at = rows_j[:, :1] * spans
    chosen = jnp.zeros((1, LANES), F32)
    for home in range(spans):
        chosen += jnp.sum(jnp.where(span_at + home == held, told[home].astype(F32), 0.0), axis=0, keepdims=True)
    count = lane_sum(lane == positions + 1, chosen)
    owner = jnp.floor((chosen + 0.5) * (1.0 / vocab))
    column = to_column(owner * TILE, positions)
    place_lane = lax.broadcasted_iota(jnp.int32, (part, shards * TILE), 1).astype(F32)
    for g in range(sections):
        for h in range(heads):
            r = g * heads + h
            picks[r * part : (r + 1) * part, :] = (
                (place_lane == column[g * part : (g + 1) * part] + r).astype(F32).astype(BF16)
            )

    wait_in(condition.at[pl.ds(0, mps - 1)], cond_sems.at[1])
    wait_in(arrived.at[pl.ds(1, shards - 1)], row_sems.at[1])

    cond = condition[...].reshape(span_len, enc_width)
    rows_in = arrived[...].reshape(shards * TILE, LANES)
    over_x = []
    for g in range(sections):
        embedded = jnp.dot(
            picks[g * heads * part : (g + 1) * heads * part, :], rows_in, preferred_element_type=F32
        )
        embedded_bf16 = embedded.astype(BF16)
        scores = []
        for h in range(heads):
            scores.append(
                lax.dot_general(
                    embedded_bf16[h * part : (h + 1) * part],
                    cond[:, h * LANES : (h + 1) * LANES],
                    (((1,), (1,)), ((), ())),
                    preferred_element_type=F32,
                )
            )
        weights = softmax(jnp.concatenate(scores, axis=0) * (1.0 / math.sqrt(LANES)))
        for h in range(heads):
            added = jnp.dot(
                weights[h * part : (h + 1) * part],
                cond[:, h * LANES : (h + 1) * LANES],
                preferred_element_type=F32,
            )
            encoded[mp, g, :, h * LANES : (h + 1) * LANES] = (
                embedded[h * part : (h + 1) * part] + added
            ).astype(BF16)
        over_x.append([])
        for dx in range(1, mps):
            copy = pltpu.make_async_remote_copy(
                src_ref=encoded.at[mp, g],
                dst_ref=encoded.at[mp, g],
                send_sem=enc_send.at[g, dx],
                recv_sem=enc_recv.at[g, dx],
                device_id=group_peer(0, dx),
                device_id_type=MESH,
            )
            copy.start()
            over_x[g].append(copy)

    width = kv_weight.shape[1] // 2
    local_heads = width // HD
    row_count = mps * part

    def project(g, weight):
        rows = encoded[:, g].reshape(row_count, enc_width)
        return jnp.dot(rows, weight[...], preferred_element_type=F32).astype(BF16)

    def attend(query, key_value):
        scores = []
        for t in range(local_heads):
            scores.append(
                jnp.concatenate(
                    [
                        lax.dot_general(
                            query[:, t * HD : (t + 1) * HD],
                            block[:, t * HD : (t + 1) * HD],
                            (((1,), (1,)), ((), ())),
                            preferred_element_type=F32,
                        )
                        for block in key_value
                    ],
                    axis=1,
                )
            )
        scores = jnp.concatenate(scores, axis=0) * (1.0 / math.sqrt(HD))
        neighbour = lax.broadcasted_iota(jnp.int32, scores.shape, 1) // row_count
        weights = softmax(jnp.where(neighbour.astype(F32) < count, scores, -jnp.inf))
        done = []
        for t in range(local_heads):
            added = [
                jnp.dot(
                    weights[t * span_len : (t + 1) * span_len, n * row_count : (n + 1) * row_count],
                    block[:, width + t * HD : width + (t + 1) * HD],
                    preferred_element_type=F32,
                )
                for n, block in enumerate(key_value)
            ]
            done.append(functools.reduce(jnp.add, added).astype(BF16))
        return jnp.concatenate(done, axis=1)

    for copy in pair_copies:
        copy.wait_recv()
    theirs, ours = [], []
    for g in range(sections):
        for copy in over_x[g]:
            copy.wait_recv()
        theirs.append(project(g, kv_other))
        if g + 1 < sections:
            ours.append(project(g, kv_weight))
    reply[...] = attend(queries_other[...], theirs)
    pair_copies.append(pair_copy(2, reply, given))
    ours.append(project(sections - 1, kv_weight))
    out[own_rows, :] = attend(queries[own_rows, :], ours)

    wait_out(facts.at[0, pl.ds(0, (shards - 1) * spans)], facts_sems.at[rings])
    wait_out(arrived.at[pl.ds(1, shards - 1)], row_sems.at[0])
    wait_out(partial_out.at[pl.ds(1, groups - 1)], part_sems.at[0])
    wait_out(condition.at[pl.ds(1, mps - 1)], cond_sems.at[0])
    for copy in sum(over_x, []) + pair_copies:
        copy.wait_send()
    pair_copies[-1].wait_recv()
    out[other_rows, :] = given[...]


def softmax(scores):
    high = jnp.max(scores, axis=1, keepdims=True)
    raised = jnp.exp(scores - high)
    return (raised / jnp.sum(raised, axis=1, keepdims=True)).astype(BF16)


def per_device(
    mesh_shape, span_states, queries, slot_span, neighbour_ids, neighbour_count, table, cond_weight, kv_weight
):
    shards, sections, mps = mesh_shape["seq"], mesh_shape["section"], mesh_shape["mp"]
    groups = sections * mps
    spans = slot_span.shape[0]
    part = neighbour_ids.shape[1] // groups
    tokens, width = queries.shape
    vocab, enc_width = table.shape
    pairs = 2 * width // LANES
    kv_rows = (
        kv_weight.reshape(enc_width, 2, width // LANES, LANES)
        .transpose(0, 2, 1, 3)
        .reshape(enc_width * pairs, LANES)
    )
    line = jnp.concatenate([slot_span, neighbour_count])
    line = jnp.pad(line, (0, neighbour_ids.shape[1] - line.shape[0]))
    own_info = jnp.concatenate([neighbour_ids, line[None]], axis=0)
    vmem = pl.BlockSpec(memory_space=pltpu.VMEM)
    hbm = pl.BlockSpec(memory_space=pltpu.HBM)
    rows_out = groups // mps * (enc_width // LANES)
    block_rows = tokens // groups
    span_len = tokens // spans
    dma = pltpu.SemaphoreType.DMA
    return pl.pallas_call(
        functools.partial(kernel, (shards, sections, mps, spans, part, span_len)),
        out_shape=jax.ShapeDtypeStruct(queries.shape, queries.dtype),
        in_specs=[vmem] + [hbm] * 5,
        out_specs=vmem,
        scratch_shapes=[
            pltpu.VMEM(span_states.shape, BF16),
            pltpu.VMEM(queries.shape, BF16),
            pltpu.VMEM((span_len, width), BF16),
            pltpu.VMEM(table.shape, BF16),
            pltpu.VMEM(cond_weight.shape, BF16),
            pltpu.VMEM(kv_rows.shape, BF16),
            pltpu.VMEM((enc_width, 2 * width), BF16),
            pltpu.VMEM((enc_width, 2 * width), BF16),
            pltpu.VMEM((enc_width // 8 * pairs, LANES), F32),
            pltpu.VMEM((RINGS, shards * spans, LANES), jnp.int32),
            pltpu.VMEM((shards // RINGS * TILE, LANES), F32),
            pltpu.VMEM((RINGS, shards // RINGS, TILE, LANES), BF16),
            pltpu.VMEM((shards, TILE, LANES), BF16),
            pltpu.VMEM((rows_out * part, shards * TILE), BF16),
            pltpu.VMEM((groups, block_rows, enc_width), F32),
            pltpu.VMEM((groups, block_rows, enc_width), BF16),
            pltpu.VMEM((groups, block_rows, enc_width), BF16),
            pltpu.VMEM((mps, block_rows, enc_width), BF16),
            pltpu.VMEM((mps, sections, part, enc_width), BF16),
            pltpu.VMEM((span_len, width), BF16),
            pltpu.VMEM((span_len, width), BF16),
            dma((5,)),
            dma((RINGS + 1,)),
            dma((2,)),
            dma((2,)),
            dma((2,)),
            dma((sections, mps)),
            dma((sections, mps)),
            dma((3,)),
            dma((3,)),
        ],
        compiler_params=pltpu.CompilerParams(
            collective_id=0, has_side_effects=True, vmem_limit_bytes=(53 * 1024 + 768) * 1024
        ),
    )(own_info, span_states, queries, table, cond_weight, kv_rows)


def solution(mesh):
    placed = (
        P("seq", ("section", "mp")),
        P("seq", ("section", "mp")),
        P("seq"),
        P("seq", None),
        P("seq"),
        P("seq", None),
        P(("section", "mp"), None),
        P(None, None, ("section", "mp")),
    )
    return jax.shard_map(
        functools.partial(per_device, dict(mesh.shape)),
        mesh=mesh,
        in_specs=placed,
        out_specs=P("seq", ("section", "mp")),
        check_vma=False,
    )
```
